32 devices in a mesh: seq: 8 (over z, x), tensor: 4 (over y, core).
Axes of the slice: x: 2, y: 2, z: 4, core: 2. Of those that a mesh axis runs over, the one named last changes fastest.
Arguments:
- queries: bfloat16 [1024, 32, 128], P('seq', 'tensor'), may hold values from -6 to 6
- keys: bfloat16 [2, 1024, 32, 128], P(None, 'seq', 'tensor'), may hold values from -6 to 6
- values: bfloat16 [2, 1024, 32, 128], P(None, 'seq', 'tensor'), may hold values from -24 to 24
- beta: float32 [2, 32, 1024], P(None, 'tensor', 'seq'), may hold values from 0.25 to 2
- decay: float32 [32, 1024], P('tensor', 'seq'), may hold values from -0.75 to 0
- out_gain: float32 [128], replicated, may hold values from 0.1 to 1.9
- residual: bfloat16 [1024, 4096], P('seq', 'tensor'), may hold values from -40 to 40
- ffn_gain: float32 [4096], replicated, may hold values from 0.1 to 1.9
- up_blocks: bfloat16 [64, 16, 128, 128], P('tensor'), may hold values from -0.125 to 0.125
- up_index: int32 [64, 16], P('tensor'), may hold values from 0 to 31, as said below
- down_kept_tiles: bfloat16 [64, 16, 128, 128], P('tensor'), may hold values from -0.09375 to 0.09375
- down_index: int32 [64, 16], P('tensor'), may hold values from 0 to 31, as said below
Outputs:
- layer_out: bfloat16 [1024, 4096], P('seq', 'tensor')
The draws below stay inside these ranges and needn't reach their ends.
Inputs may be any that keep to these rules, and one draw needn't show every extreme that they name: `up_index`: each row names 16 different tiles. `down_index`: each row names 16 different tiles.
All inputs are finite; a program needn't handle non-finite values.
Results may differ from the reference program's by a relative error of at most 0.014.
Values may be sent and summed in bfloat16 or wider, within the bound.
No kernel may reach another device: no remote copies, remote signals or barrier semaphores. Data moves between devices by JAX's collectives and lax.ppermute only.
A program may use at most 128 MiB of HBM per device.

```python
import math
import jax
import jax.numpy as jnp
from jax import lax

HEADS = 32
DK = 128
D = 4096
FF = 8192
TILE = 128
BLOCK_TOK = 64
TOK_DEV = 128
TOKENS = 1024
NTILE = 32
HTILE = 64
KEEP = 16
N_TENSOR = 4


def head_class(key):
    ranking = jax.random.permutation(jax.random.fold_in(key, 11), HEADS)
    first_cut = HEADS // 2
    second_cut = HEADS // 2 + HEADS // 8
    third_cut = HEADS // 2 + HEADS // 4
    kind = (ranking >= first_cut).astype(jnp.int32) + (ranking >= second_cut).astype(jnp.int32) + (ranking >= third_cut).astype(jnp.int32)
    return kind


def draw_decay(key, part):
    kind = head_class(key)
    streams = jax.random.split(jax.random.fold_in(key, 23), 5)
    device_rate = jnp.exp(jax.random.uniform(streams[0], (HEADS, TOKENS // TOK_DEV), minval=math.log(0.5), maxval=math.log(2.0)))
    device_rate = jnp.repeat(device_rate, TOK_DEV, axis=1)
    rough = jnp.exp(jax.random.uniform(streams[1], (HEADS, TOKENS), minval=math.log(0.7), maxval=math.log(1.4)))
    fast_rate = jnp.exp(jax.random.uniform(streams[2], (HEADS, 1), minval=math.log(1.0 / 50.0), maxval=math.log(1.0 / 30.0)))
    slow_rate = 0.5 / TOKENS
    middle_rate = 0.4 / TOK_DEV
    base_rate = jnp.where(kind[:, None] <= 1, slow_rate, jnp.where(kind[:, None] == 2, middle_rate, fast_rate))
    speed_ratio = base_rate * device_rate * rough
    slot_positions = jax.random.randint(streams[3], (HEADS, 2), 0, TOKENS)
    tile_locations = jnp.arange(TOKENS, dtype=jnp.int32)
    sudden_count = (tile_locations[None, :] == slot_positions[:, 0:1]) | (tile_locations[None, :] == slot_positions[:, 1:2])
    discard_fraction = jnp.log(jax.random.uniform(streams[4], (HEADS, TOKENS), minval=0.5, maxval=0.8))
    return jnp.where(sudden_count, discard_fraction, -speed_ratio).astype(jnp.float32)


def draw_beta(key, part):
    kind = head_class(key)
    streams = jax.random.split(jax.random.fold_in(key, 37), 3)
    margin = 32.0 / TOKENS * jnp.exp(jax.random.uniform(streams[0], (2, HEADS, TOKENS), minval=math.log(0.5), maxval=math.log(2.0)))
    quick = jax.random.uniform(streams[1], (2, HEADS, TOKENS), minval=0.3, maxval=1.7)
    gentle = jax.random.uniform(streams[2], (2, HEADS, TOKENS), minval=0.25, maxval=0.45)
    kind_all = kind[None, :, None]
    chosen = jnp.where((kind_all == 0) | (kind_all == 2), 2.0 - margin, jnp.where(kind_all == 1, gentle, quick))
    return chosen.astype(jnp.float32)


def draw_values(key, part):
    streams = jax.random.split(jax.random.fold_in(key, 61), 2)
    base = jax.random.truncated_normal(streams[0], -4.0, 4.0, (2, TOKENS, HEADS, DK))
    block_scale = jnp.exp(jax.random.uniform(streams[1], (TOKENS // BLOCK_TOK, HEADS), minval=math.log(0.15), maxval=math.log(6.0)))
    block_scale = jnp.repeat(block_scale, BLOCK_TOK, axis=0)
    return (base * block_scale[None, :, :, None]).astype(jnp.bfloat16)


def draw_residual(key, part):
    streams = jax.random.split(jax.random.fold_in(key, 53), 3)
    base = jax.random.truncated_normal(streams[0], -4.0, 4.0, (TOKENS, D))
    row_scale = jnp.exp(jax.random.uniform(streams[1], (TOKENS, 1), minval=math.log(0.3), maxval=math.log(3.0)))
    columns = jnp.arange(D, dtype=jnp.float32) / (D - 1)
    col_scale = jnp.exp(math.log(3.0) * columns)[None, :] / math.sqrt(3.0)
    col_scale = col_scale * jnp.exp(jax.random.uniform(streams[2], (1, D), minval=-0.35, maxval=0.35))
    return (base * row_scale * col_scale).astype(jnp.bfloat16)


def pick_tiles(key):
    scores = jax.random.randint(key, (HTILE, NTILE), 0, 1 << 20) * NTILE + jnp.arange(NTILE, dtype=jnp.int32)[None, :]
    _, chosen = lax.top_k(scores, KEEP)
    return chosen.astype(jnp.int32)


def draw_up_index(key, part):
    return pick_tiles(jax.random.fold_in(key, 41))


def draw_down_index(key, part):
    return pick_tiles(jax.random.fold_in(key, 43))


def level_of(key, extent, cuts, low, high):
    gain = 1.0
    for axis_at, parts in cuts:
        steps = jax.random.uniform(jax.random.fold_in(jax.random.fold_in(key, 6), axis_at), (parts,), jnp.float32, low / len(cuts), high / len(cuts))
        gain = gain * jnp.repeat(jnp.exp(steps), extent[axis_at] // parts).reshape((-1,) + (1,) * (len(extent) - 1 - axis_at))
    return gain


def bell_draw(rng, extent, spread, most, cuts=(), held_as=jnp.bfloat16):
    values = spread * jax.random.normal(rng, extent, jnp.float32)
    if cuts:
        values = values * level_of(rng, extent, cuts, -0.22, 0.18)
    return jnp.clip(values, -most, most).astype(held_as)


def setup_inputs(seed: int = 0) -> dict:
    key_of = jax.random.split(jax.random.key(seed), 13)
    queries = bell_draw(key_of[0], (TOKENS, HEADS, DK), 1.0, 6.0, ((0, 8), (1, 4)))
    keys = bell_draw(key_of[1], (2, TOKENS, HEADS, DK), 1.0, 6.0, ((1, 8), (2, 4)))
    values = draw_values(jax.random.fold_in(key_of[12], 71), 0)
    beta = draw_beta(jax.random.fold_in(key_of[12], 71), 0)
    decay = draw_decay(jax.random.fold_in(key_of[12], 71), 0)
    out_gain = jnp.clip(1.0 + 0.18 * jax.random.normal(key_of[5], (DK,), jnp.float32), 0.1, 1.9)
    residual = draw_residual(jax.random.fold_in(key_of[12], 71), 0)
    ffn_gain = jnp.clip(1.0 + 0.18 * jax.random.normal(key_of[7], (D,), jnp.float32), 0.1, 1.9)
    up_blocks = bell_draw(key_of[8], (HTILE, KEEP, TILE, TILE), (KEEP * TILE) ** -0.5, 0.125, ((0, 4),))
    up_index = draw_up_index(jax.random.fold_in(key_of[12], 71), 0)
    down_kept_tiles = bell_draw(key_of[10], (HTILE, KEEP, TILE, TILE), (FF // 2) ** -0.5, 0.09375, ((0, 4),))
    down_index = draw_down_index(jax.random.fold_in(key_of[12], 71), 0)
    return {"queries": queries, "keys": keys, "values": values, "beta": beta, "decay": decay, "out_gain": out_gain, "residual": residual, "ffn_gain": ffn_gain, "up_blocks": up_blocks, "up_index": up_index, "down_kept_tiles": down_kept_tiles, "down_index": down_index}


def normed(given):
    wide = given.astype(jnp.float32)
    return wide * lax.rsqrt(lax.optimization_barrier(jnp.sum(wide * wide, -1, keepdims=True)) + 1e-06)

def reference(queries, keys, values, beta, decay, out_gain, residual, ffn_gain, up_blocks, up_index, down_kept_tiles, down_index):
    highest = lax.Precision.HIGHEST
    query_unit = normed(queries)
    key_unit = normed(keys).transpose(1, 0, 2, 3)
    value_all = values.astype(jnp.float32).transpose(1, 0, 2, 3)
    beta_all = beta.transpose(2, 0, 1)
    gate_all = jnp.exp(decay).T

    def advance(state, inputs):
        query_now, key_now, value_now, beta_now, gate_now = inputs
        state = gate_now[:, None, None] * state
        for factor in range(2):
            key_one = key_now[factor]
            read_out = jnp.einsum('hd,hde->he', key_one, state, precision=highest)
            update = value_now[factor] - read_out
            state = state + beta_now[factor][:, None, None] * key_one[:, :, None] * update[:, None, :]
        result = jnp.einsum('hd,hde->he', query_now, state, precision=highest)
        return (state, result)
    start = jnp.zeros((HEADS, DK, DK), jnp.float32)
    _, head_out = lax.scan(advance, start, (query_unit, key_unit, value_all, beta_all, gate_all))
    normed_out = head_out * lax.rsqrt(lax.optimization_barrier(jnp.mean(head_out * head_out, -1, keepdims=True)) + 1e-05) * out_gain
    hidden_state = (residual.astype(jnp.float32) + normed_out.reshape(TOKENS, D)).astype(jnp.bfloat16)
    hidden_wide = hidden_state.astype(jnp.float32)
    ffn_in = (hidden_wide * lax.rsqrt(lax.optimization_barrier(jnp.mean(hidden_wide * hidden_wide, -1, keepdims=True)) + 1e-05) * ffn_gain).astype(jnp.bfloat16)
    tiles_in = ffn_in.astype(jnp.float32).reshape(TOKENS, NTILE, TILE)
    group_tiles = HTILE // N_TENSOR
    up_group = up_blocks.reshape(N_TENSOR, group_tiles, KEEP, TILE, TILE)
    up_place = up_index.reshape(N_TENSOR, group_tiles, KEEP)
    down_group = down_kept_tiles.reshape(N_TENSOR, group_tiles, KEEP, TILE, TILE)
    down_place = down_index.reshape(N_TENSOR, group_tiles, KEEP)
    tile_ids = jnp.arange(NTILE, dtype=jnp.int32)

    def one_group(total, inputs):
        up_part, up_ids, down_part, down_ids = inputs
        picked = jnp.take(tiles_in, up_ids, axis=1)
        pre_act = jnp.einsum('tcjd,cjdh->tch', picked, up_part.astype(jnp.float32), precision=highest)
        activation = lax.optimization_barrier(jax.nn.gelu(pre_act).astype(jnp.bfloat16)).astype(jnp.float32)
        contrib = jnp.einsum('tch,cjho->tcjo', activation, down_part.astype(jnp.float32), precision=highest)
        one_hot = (down_ids[:, :, None] == tile_ids[None, None, :]).astype(jnp.float32)
        group_sum = jnp.einsum('tcjo,cjb->tbo', contrib, one_hot, precision=highest)
        group_sum = lax.optimization_barrier(group_sum.astype(jnp.bfloat16)).astype(jnp.float32)
        return (total + group_sum, None)
    ffn_out, _ = lax.scan(one_group, jnp.zeros((TOKENS, NTILE, TILE), jnp.float32), (up_group, up_place, down_group, down_place))
    return (hidden_wide + ffn_out.reshape(TOKENS, D)).astype(jnp.bfloat16)
```

```python
import functools

import jax
import jax.numpy as jnp
from jax import lax
from jax.experimental import pallas as pl
from jax.experimental.pallas import tpu as pltpu
from jax.sharding import PartitionSpec as P

F32 = jnp.float32
BF16 = jnp.bfloat16
HEAD_GROUP = 4
MIB = 1 << 20
VMEM = pl.BlockSpec(memory_space=pltpu.VMEM)
SMEM = pl.BlockSpec(memory_space=pltpu.SMEM)
ANY = pl.BlockSpec(memory_space=pl.ANY)


def dot(a, b):
    return jnp.dot(a, b, preferred_element_type=F32)


def dot_nt(a, b):
    return lax.dot_general(a, b, (((1,), (1,)), ((), ())), preferred_element_type=F32)


def dot_tn(a, b):
    return lax.dot_general(a, b, (((0,), (0,)), ((), ())), preferred_element_type=F32)


def split(x):
    high = x.astype(BF16)
    return high, (x - high.astype(F32)).astype(BF16)


def dot_wide(a, b):
    width = a[0].shape[1]
    row = jnp.concatenate([b[0], b[1]], 1)
    out = dot(jnp.concatenate([a[0], a[1]], 1), jnp.concatenate([row, row], 0))
    return out[:, :width] + out[:, width:]


def column(row):
    n = row.shape[1]
    return jnp.broadcast_to(row, (n, n)).T


def head_rows(ref, h, stride):
    return ref[pl.ds(h, ref.shape[0] // stride, stride=stride), :]


def stacked(first, second):
    half = first.shape[0] // 2
    return [
        jnp.concatenate([first[i * half : (i + 1) * half], second[i * half : (i + 1) * half]], 0)
        for i in range(2)
    ]


def running_rows(decay_ref):
    tokens = decay_ref.shape[1]
    earlier = lax.broadcasted_iota(jnp.int32, (tokens, tokens), 0)
    later = lax.broadcasted_iota(jnp.int32, (tokens, tokens), 1)
    return jnp.dot(
        decay_ref[...],
        (earlier <= later).astype(F32),
        preferred_element_type=F32,
        precision=lax.Precision.HIGHEST,
    )


def doubled(rows, half):
    return [
        jnp.concatenate([rows[:, i * half : (i + 1) * half]] * 2, 1) for i in range(2)
    ]


def terms_kernel(exchange, beta_ref, decay_ref, k_ref, v_ref, *refs):
    heads, tokens = decay_ref.shape
    width = k_ref.shape[-1]
    half = tokens // 2
    span = 2 * half
    out_refs, sol_ref = refs[:heads], refs[heads]
    k_all, v_all, row_ref = refs[heads + 1 :]
    me = lax.axis_index("seq") if exchange else 0
    for j in range(2):
        k_all[j] = k_ref[j].astype(F32).reshape(tokens * heads, width)
        v_all[j] = v_ref[j].astype(F32).reshape(tokens * heads, width)
    run = running_rows(decay_ref)
    run_half = doubled(run, half)
    beta_half = stacked_beta(beta_ref, half)
    last = jnp.broadcast_to(run[:, tokens - 1 :], (heads, span))
    for i in range(2):
        row_ref[i] = run_half[i]
        row_ref[2 + i] = beta_half[i]
    row_ref[4] = last

    row_at = lax.broadcasted_iota(jnp.int32, (span, span), 0)
    col_at = lax.broadcasted_iota(jnp.int32, (span, span), 1)
    row_time = 2 * lax.rem(row_at, half) + row_at // half
    col_time = 2 * lax.rem(col_at, half) + col_at // half
    below = col_time < row_time
    apart = jnp.where(below, row_time ^ col_time, 0)
    eye = (row_at == col_at).astype(F32)
    eye_wide = eye[:width, :width]
    left = col_at < half

    for start in range(0, heads, HEAD_GROUP):
        slots = range(start, min(start + HEAD_GROUP, heads))
        chains = []
        for s in slots:
            h = lax.rem(me + s, heads)
            keys = stacked(*(head_rows(k_all.at[j], h, heads) for j in range(2)))
            values = stacked(*(head_rows(v_all.at[j], h, heads) for j in range(2)))
            keys = [x.astype(BF16) for x in keys]
            values = [x.astype(BF16) for x in values]
            run_row = [row_ref[i, pl.ds(h, 1), :] for i in range(2)]
            beta_row = [row_ref[2 + i, pl.ds(h, 1), :] for i in range(2)]
            run_col = [column(x) for x in run_row]
            beta_col = [column(x) for x in beta_row]
            last_row = row_ref[4, pl.ds(h, 1), :]
            grams = [dot_nt(x, x) for x in keys]
            inv_row = [lax.rsqrt(jnp.sum(g * eye, 0, keepdims=True) + 1e-06) for g in grams]
            inv_col = [lax.rsqrt(jnp.sum(g * eye, 1, keepdims=True) + 1e-06) for g in grams]
            lowers, inverses = [], []
            for i in range(2):
                spread = jnp.exp(jnp.where(below, run_col[i] - run_row[i], 0.0))
                scaled = grams[i] * inv_row[i] * inv_col[i]
                lower = jnp.where(below, beta_col[i] * spread * scaled, 0.0)
                pair = jnp.where(apart == 1, lower, 0.0)
                step = jnp.where((apart >= 2) & (apart < 4), lower, 0.0)
                by_row = jnp.sum(pair, 1, keepdims=True)
                by_col = jnp.sum(pair, 0, keepdims=True)
                step = jnp.concatenate(
                    [step[:half], step[half:] - by_row[half:] * step[:half]], 0
                )
                swapped = jnp.concatenate([step[:, half:], step[:, :half]], 1)
                step = step - jnp.where(left, swapped * by_col, 0.0)
                lowers.append(lower)
                inverses.append(eye - pair - step)
            cross = dot_nt(keys[1], keys[0]) * inv_row[0] * inv_col[1]
            cross = cross * beta_col[1] * jnp.exp(run_col[1] - run_row[0])
            chains.append(
                dict(
                    s=s, keys=keys, values=values, run_row=run_row, beta_row=beta_row,
                    run_col=run_col, last_row=last_row, inv_row=inv_row, inv_col=inv_col,
                    lowers=lowers, inverses=inverses, cross=cross,
                )
            )
        size = 4
        while size < span:
            for c in chains:
                c["parts"] = [split(x) for x in c["inverses"]]
                c["middle"] = [
                    dot_wide(
                        split(jnp.where((apart >= size) & (apart < 2 * size), low, 0.0)), part
                    )
                    for low, part in zip(c["lowers"], c["parts"])
                ]
            for c in chains:
                c["inverses"] = [
                    x - dot_wide(part, split(mid))
                    for x, part, mid in zip(c["inverses"], c["parts"], c["middle"])
                ]
            size *= 2
        for c in chains:
            c["parts"] = [split(x) for x in c["inverses"]]
            c["middle"] = dot_wide(split(c["cross"]), c["parts"][0])
        for c in chains:
            c["corner"] = -dot_wide(c["parts"][1], split(c["middle"]))
        for c in chains:
            scale_v = c["beta_row"]
            scale_k = [
                b * jnp.exp(r) * n for b, r, n in zip(c["beta_row"], c["run_row"], c["inv_row"])
            ]
            solved = []
            for scale, source in ((scale_k, c["keys"]), (scale_v, c["values"])):
                first = split(c["inverses"][0] * scale[0])
                upper = dot(jnp.concatenate(first, 1), jnp.concatenate([source[0]] * 2, 0))
                corner = split(c["corner"] * scale[0])
                second = split(c["inverses"][1] * scale[1])
                both = jnp.concatenate(source, 0)
                lower = dot(jnp.concatenate([corner[0], second[0]], 1), both) + dot(
                    jnp.concatenate([corner[1], second[1]], 1), both
                )
                solved.append((upper, lower))
            rows = [jnp.concatenate([solved[0][i], solved[1][i]], 1) for i in range(2)]
            c["rows"] = rows
            for i in range(2):
                sol_ref[c["s"], i * span : (i + 1) * span, :] = rows[i]
        for c in chains:
            last_col = column(c["last_row"])
            weighted = []
            for i in range(2):
                remain = jnp.exp(last_col - c["run_col"][i]) * c["inv_col"][i]
                weighted.append(c["rows"][i] * jnp.concatenate([remain, remain], 1))
            high, low = split(jnp.concatenate(weighted, 0))
            keys = jnp.concatenate(c["keys"], 0)
            ends = dot_tn(keys, high) + dot_tn(keys, low)
            gate = jnp.exp(c["last_row"])
            trans = eye_wide * gate - ends[:, :width]
            out_refs[c["s"]][...] = jnp.concatenate([trans, ends[:, width:]], 1).astype(BF16)


def stacked_beta(beta_ref, half):
    first, second = beta_ref[0], beta_ref[1]
    return [
        jnp.concatenate(
            [first[:, i * half : (i + 1) * half], second[:, i * half : (i + 1) * half]], 1
        )
        for i in range(2)
    ]


def mixing_kernel(exchange, decay_ref, q_ref, k_ref, sol_ref, out_ref, q_all, k_all, run_ref):
    heads, tokens = decay_ref.shape
    width = k_ref.shape[-1]
    half = tokens // 2
    span = 2 * half
    me = lax.axis_index("seq") if exchange else 0
    q_all[...] = q_ref[...].astype(F32).reshape(tokens * heads, width)
    for j in range(2):
        k_all[j] = k_ref[j].astype(F32).reshape(tokens * heads, width)
    run_ref[...] = running_rows(decay_ref)
    token_at = lax.broadcasted_iota(jnp.int32, (tokens, 2 * span), 0)
    row_at = lax.broadcasted_iota(jnp.int32, (tokens, 2 * span), 1)
    seen = (row_at // span) * half + lax.rem(row_at, half) <= token_at
    row_at = lax.broadcasted_iota(jnp.int32, (span, span), 0)
    col_at = lax.broadcasted_iota(jnp.int32, (span, span), 1)
    eye = (row_at == col_at).astype(F32)

    def one_head(s, carry):
        h = lax.rem(me + s, heads)
        queries = head_rows(q_all, h, heads)
        keys = stacked(*(head_rows(k_all.at[j], h, heads) for j in range(2)))
        run = run_ref[pl.ds(h, 1), :]
        run_col = column(run)
        run_row = jnp.concatenate(doubled(run, half), 1)
        keys = [x.astype(BF16) for x in keys]
        inv_row = [
            lax.rsqrt(jnp.sum(dot_nt(x, x) * eye, 0, keepdims=True) + 1e-06) for x in keys
        ]
        inv_q = lax.rsqrt(jnp.sum(queries * queries, 1, keepdims=True) + 1e-06)
        inner = dot_nt(queries.astype(BF16), jnp.concatenate(keys, 0))
        spread = jnp.concatenate([run_col, run_col], 1) - run_row
        mixing = inner * inv_q * jnp.concatenate(inv_row, 1)
        mixing = jnp.where(seen, jnp.exp(jnp.where(seen, spread, 0.0)) * mixing, 0.0)
        mix_high, mix_low = split(mixing)
        sol_high, sol_low = split(sol_ref[s])
        mixed = dot(mix_high, sol_high) + dot(mix_low, sol_high) + dot(mix_high, sol_low)
        tilde = jnp.exp(run_col) * (queries * inv_q) - mixed[:, :width]
        out_ref[s] = jnp.concatenate([tilde, mixed[:, width:]], 1)
        return carry

    lax.fori_loop(0, heads, one_head, 0, unroll=2)


def chain_kernel(count, *refs):
    held = refs[2 * count]
    width = refs[0].shape[0]
    me = lax.axis_index("seq")
    for s in range(count):
        held[s] = refs[s][...]
    outs = refs[2 * count + 1]
    state = jnp.zeros((width, width), F32)
    for k in range(count):
        outs[lax.rem(k - me + count, count)] = state.astype(BF16)
        if k + 1 < count:
            block = held[lax.rem(me - k + count, count)]
            high, low = split(state)
            both = dot(block[:, :width], jnp.concatenate([high, low], 1))
            state = both[:, :width] + both[:, width:] + block[:, width:].astype(F32)
    for s in range(count):
        refs[count + s][...] = outs[s]


def emit_kernel(exchange, mixed_ref, gain_ref, residual_ref, *refs):
    heads = mixed_ref.shape[0]
    width = mixed_ref.shape[2] // 2
    state_refs, out_ref, row_all = refs[:heads], refs[heads], refs[heads + 1]
    me = lax.axis_index("seq") if exchange else 0
    for s in range(heads):
        row_all[s] = state_refs[s][...]
    for h in range(heads):
        slot_terms = lax.rem(h - me + heads, heads) if exchange else h
        slot_state = lax.rem(me - h + heads, heads) if exchange else h
        mixed = mixed_ref[slot_terms]
        high, low = split(mixed[:, :width])
        state = row_all[slot_state]
        out = dot(
            jnp.concatenate([high, low], 1), jnp.concatenate([state, state], 0)
        ) + mixed[:, width:]
        scale = lax.rsqrt(jnp.mean(out * out, 1, keepdims=True) + 1e-05)
        out = out * scale * gain_ref[...]
        out_ref[h] = (residual_ref[:, h * width : (h + 1) * width].astype(F32) + out).astype(BF16)


def ffn_kernel(count, gain_ref, up_at, down_at, up_hbm, down_hbm, *refs):
    parts, outs = refs[:count], refs[count : 2 * count]
    tiles_in, act, total, up_ref, down_ref, up_sem, down_sem = refs[2 * count :]
    groups, kept, side, _ = up_hbm.shape
    tiles, tokens, _ = tiles_in.shape
    each = tiles // count
    me = lax.axis_index("tensor")
    ups = [pltpu.make_async_copy(up_hbm.at[c], up_ref.at[c], up_sem.at[c]) for c in range(groups)]
    downs = [
        pltpu.make_async_copy(down_hbm.at[c], down_ref.at[c], down_sem.at[c]) for c in range(groups)
    ]
    for copy in ups + downs:
        copy.start()
    squares = jnp.zeros((tokens, side), F32)
    for part in parts:
        for b in range(each):
            wide = part[b].astype(F32)
            squares += wide * wide
    scale = lax.rsqrt(jnp.sum(squares, 1, keepdims=True) / (tiles * side) + 1e-05)
    for m, part in enumerate(parts):
        base = (me ^ m) * each
        for b in range(each):
            gain = gain_ref[pl.ds(base + b, 1), :]
            tiles_in[base + b] = (part[b].astype(F32) * scale * gain).astype(BF16)
    for c in range(groups):
        ups[c].wait()
        picked = jnp.concatenate([tiles_in[up_at[c, j]] for j in range(kept)], 1)
        pre = dot(picked, up_ref[c].reshape(kept * side, side))
        act[c] = jax.nn.gelu(pre).astype(BF16)
    total[...] = jnp.zeros_like(total)
    for c in range(groups):
        downs[c].wait()
        now = act[c]
        for j in range(0, kept, 2):
            both = dot(now, jnp.concatenate([down_ref[c, j], down_ref[c, j + 1]], 1))
            total[down_at[c, j]] += both[:, :side]
            total[down_at[c, j + 1]] += both[:, side:]
    for m, out in enumerate(outs):
        base = (me ^ m) * each
        out[...] = total[pl.ds(base, each)].astype(BF16)


def final_kernel(hidden_ref, *refs):
    out_ref = refs[-1]
    tiles, _, side = hidden_ref.shape
    for b in range(tiles):
        total = refs[0][b].astype(F32)
        for ref in refs[1:-1]:
            total += ref[b].astype(F32)
        out_ref[:, b * side : (b + 1) * side] = (hidden_ref[b].astype(F32) + total).astype(BF16)


def local_call(kernel, out_shape, ins, args, scratch=(), flops=0, moved=0, limit=48 * MIB):
    return pl.pallas_call(
        kernel,
        out_shape=out_shape,
        in_specs=ins,
        out_specs=jax.tree.map(lambda _: VMEM, out_shape),
        scratch_shapes=scratch,
        compiler_params=pltpu.CompilerParams(vmem_limit_bytes=limit),
        cost_estimate=pl.CostEstimate(flops=flops, bytes_accessed=moved, transcendentals=0),
    )(*args)


def prefix_states(terms):
    count, index = lax.axis_size("seq"), lax.axis_index("seq")
    everything = lax.all_gather(jnp.stack(terms), "seq")
    width = terms[0].shape[0]

    def step(k, state):
        block = everything[k]
        new = jnp.einsum(
            "hde,hef->hdf",
            block[..., :width].astype(F32),
            state,
            precision=lax.Precision.HIGHEST,
        ) + block[..., width:].astype(F32)
        return jnp.where(k < index, new, state)

    start = jnp.zeros((len(terms), width, width), F32)
    states = lax.fori_loop(0, count, step, start).astype(BF16)
    return [states[h] for h in range(len(terms))]


def per_device(
    queries, keys, values, beta, decay, out_gain, residual, ffn_gain,
    up_blocks, up_index, down_kept_tiles, down_index,
):
    tokens, heads, width = queries.shape
    seq_count, tensor_count = lax.axis_size("seq"), lax.axis_size("tensor")
    exchange = seq_count == heads
    span = tokens
    term = jax.ShapeDtypeStruct((width, 2 * width), BF16)
    *terms, solved = local_call(
        functools.partial(terms_kernel, exchange),
        [term] * heads + [jax.ShapeDtypeStruct((heads, 2 * span, 2 * width), F32)],
        [VMEM] * 4,
        (beta, decay, keys, values),
        [
            pltpu.VMEM((2, tokens * heads, width), F32),
            pltpu.VMEM((2, tokens * heads, width), F32),
            pltpu.VMEM((5, heads, span), F32),
        ],
        flops=5_000_000_000,
    )
    mixed = local_call(
        functools.partial(mixing_kernel, exchange),
        jax.ShapeDtypeStruct((heads, tokens, 2 * width), F32),
        [VMEM] * 4,
        (decay, queries, keys, solved),
        [
            pltpu.VMEM((tokens * heads, width), F32),
            pltpu.VMEM((2, tokens * heads, width), F32),
            pltpu.VMEM((heads, tokens), F32),
        ],
        flops=5_000_000_000,
    )
    if exchange:
        shifts = [[(k, (k + s) % seq_count) for k in range(seq_count)] for s in range(seq_count)]
        arrived = [terms[0]] + [
            lax.ppermute(terms[s], "seq", shifts[s]) for s in range(1, seq_count)
        ]
        state = jax.ShapeDtypeStruct((width, width), BF16)
        outgoing = local_call(
            functools.partial(chain_kernel, seq_count),
            [state] * seq_count,
            [VMEM] * seq_count,
            arrived,
            [
                pltpu.VMEM((seq_count, width, 2 * width), BF16),
                pltpu.VMEM((seq_count, width, width), BF16),
            ],
        )
        states = [outgoing[0]] + [
            lax.ppermute(outgoing[s], "seq", shifts[s]) for s in range(1, seq_count)
        ]
    else:
        states = prefix_states(terms)
    hidden = local_call(
        functools.partial(emit_kernel, exchange),
        jax.ShapeDtypeStruct((heads, tokens, width), BF16),
        [VMEM] * (3 + heads),
        (mixed, out_gain.reshape(1, width), residual, *states),
        [pltpu.VMEM((heads, width, width), BF16)],
    )

    flips = {
        d: [(k, k ^ d) for k in range(tensor_count)]
        for d in (1 << b for b in range(tensor_count.bit_length() - 1))
    }
    parts = {0: hidden}
    for d in sorted(flips, reverse=True):
        for m in list(parts):
            parts[m | d] = lax.ppermute(parts[m], "tensor", flips[d])
    groups, kept, side, _ = up_blocks.shape
    tiles = heads * tensor_count
    sums = local_call(
        functools.partial(ffn_kernel, tensor_count),
        [jax.ShapeDtypeStruct((heads, tokens, side), BF16)] * tensor_count,
        [VMEM, SMEM, SMEM, ANY, ANY] + [VMEM] * tensor_count,
        (
            ffn_gain.reshape(tiles, side), up_index, down_index, up_blocks, down_kept_tiles,
            *(parts[m] for m in range(tensor_count)),
        ),
        [
            pltpu.VMEM((tiles, tokens, side), BF16),
            pltpu.VMEM((groups, tokens, side), BF16),
            pltpu.VMEM((tiles, tokens, side), F32),
            pltpu.VMEM((groups, kept, side, side), BF16),
            pltpu.VMEM((groups, kept, side, side), BF16),
            pltpu.SemaphoreType.DMA((groups,)),
            pltpu.SemaphoreType.DMA((groups,)),
        ],
    )
    held = {m: [part] for m, part in enumerate(sums)}
    for d in sorted(flips):
        for m in [m for m in held if not m & d]:
            moved = lax.ppermute(added(held.pop(m | d)), "tensor", flips[d])
            held[m].append(moved)
    return local_call(
        final_kernel,
        jax.ShapeDtypeStruct((tokens, heads * side), BF16),
        [VMEM] * (1 + len(held[0])),
        (hidden, *held[0]),
    )


def added(terms):
    if len(terms) == 1:
        return terms[0]
    return sum(term.astype(F32) for term in terms).astype(BF16)


def solution(mesh):
    placed = (
        P("seq", "tensor", None),
        P(None, "seq", "tensor", None),
        P(None, "seq", "tensor", None),
        P(None, "tensor", "seq"),
        P("tensor", "seq"),
        P(),
        P("seq", "tensor"),
        P(),
        P("tensor", None, None, None),
        P("tensor", None),
        P("tensor", None, None, None),
        P("tensor", None),
    )
    return jax.shard_map(
        per_device, mesh=mesh, in_specs=placed, out_specs=P("seq", "tensor"), check_vma=False
    )
```

```python
import functools

import jax
import jax.numpy as jnp
from jax import lax
from jax.experimental import pallas as pl
from jax.experimental.pallas import tpu as pltpu
from jax.sharding import PartitionSpec as P

F32 = jnp.float32
BF16 = jnp.bfloat16
HEAD_GROUP = 4
PER_SLOT = 2
CUTS = (2, 3)
FIRST_LIMIT = 20 * (1 << 20)
MIB = 1 << 20
VMEM = pl.BlockSpec(memory_space=pltpu.VMEM)
SMEM = pl.BlockSpec(memory_space=pltpu.SMEM)
ANY = pl.BlockSpec(memory_space=pl.ANY)


def dot(a, b):
    return jnp.dot(a, b, preferred_element_type=F32)


def dot_nt(a, b):
    return lax.dot_general(a, b, (((1,), (1,)), ((), ())), preferred_element_type=F32)


def dot_tn(a, b):
    return lax.dot_general(a, b, (((0,), (0,)), ((), ())), preferred_element_type=F32)


def split(x):
    high = x.astype(BF16)
    return high, (x - high.astype(F32)).astype(BF16)


def dot_wide(a, b):
    width = a[0].shape[1]
    row = jnp.concatenate([b[0], b[1]], 1)
    out = dot(jnp.concatenate([a[0], a[1]], 1), jnp.concatenate([row, row], 0))
    return out[:, :width] + out[:, width:]


def column(row):
    n = row.shape[1]
    return jnp.broadcast_to(row, (n, n)).T


def head_rows(ref, h, stride):
    return ref[pl.ds(h, ref.shape[0] // stride, stride=stride), :]


def stacked(first, second):
    half = first.shape[0] // 2
    return [
        jnp.concatenate([first[i * half : (i + 1) * half], second[i * half : (i + 1) * half]], 0)
        for i in range(2)
    ]


def running_rows(decay_ref):
    tokens = decay_ref.shape[1]
    earlier = lax.broadcasted_iota(jnp.int32, (tokens, tokens), 0)
    later = lax.broadcasted_iota(jnp.int32, (tokens, tokens), 1)
    return jnp.dot(
        decay_ref[...],
        (earlier <= later).astype(F32),
        preferred_element_type=F32,
        precision=lax.Precision.HIGHEST,
    )


def doubled(rows, half):
    return [
        jnp.concatenate([rows[:, i * half : (i + 1) * half]] * 2, 1) for i in range(2)
    ]


def head_of(exchange, slot, u):
    if exchange:
        return PER_SLOT * (lax.rem(lax.axis_index("seq"), exchange) ^ slot) + u
    return PER_SLOT * slot + u


def first_kernel(exchange, order, beta_hbm, decay_hbm, k_hbm, v_hbm, *refs):
    _, heads, tokens = beta_hbm.shape
    width = k_hbm.shape[-1]
    half = tokens // 2
    out_refs, (sol_ref, k_heads, v_heads, row_ref) = refs[: len(order)], refs[len(order) :][:4]
    beta_ref, decay_ref, k_ref, v_ref, k_all, v_all, sems = refs[len(order) + 4 :]
    copies = [
        pltpu.make_async_copy(source, target, sems.at[n])
        for n, (source, target) in enumerate(
            ((beta_hbm, beta_ref), (decay_hbm, decay_ref), (k_hbm, k_ref), (v_hbm, v_ref))
        )
    ]
    for copy in copies:
        copy.start()
    for copy in copies[:2]:
        copy.wait()
    run = running_rows(decay_ref)
    run_half = doubled(run, half)
    beta_half = stacked_beta(beta_ref, half)
    for i in range(2):
        row_ref[i] = run_half[i]
        row_ref[2 + i] = beta_half[i]
    row_ref[4] = jnp.broadcast_to(run[:, tokens - 1 :], (heads, 2 * half))
    row_ref[5] = run
    for copy, source, wide, target in (
        (copies[2], k_ref, k_all, k_heads),
        (copies[3], v_ref, v_all, v_heads),
    ):
        copy.wait()
        for j in range(2):
            wide[j] = source[j].astype(F32).reshape(tokens * heads, width)
        for h in range(heads):
            rows = stacked(*(head_rows(wide.at[j], h, heads) for j in range(2)))
            for i in range(2):
                target[h, i] = rows[i].astype(BF16)
    solve_heads(exchange, order, k_heads, v_heads, row_ref, out_refs, sol_ref)


def later_kernel(exchange, order, k_heads, v_heads, row_ref, *refs):
    out_refs, sol_ref = refs[: len(order)], refs[len(order)]
    solve_heads(exchange, order, k_heads, v_heads, row_ref, out_refs, sol_ref)


def solve_heads(exchange, order, k_heads, v_heads, row_ref, out_refs, sol_ref):
    span, width = k_heads.shape[2:]
    half = span // 2
    row_at = lax.broadcasted_iota(jnp.int32, (span, span), 0)
    col_at = lax.broadcasted_iota(jnp.int32, (span, span), 1)
    row_time = 2 * lax.rem(row_at, half) + row_at // half
    col_time = 2 * lax.rem(col_at, half) + col_at // half
    below = col_time < row_time
    apart = jnp.where(below, row_time ^ col_time, 0)
    eye = (row_at == col_at).astype(F32)
    eye_wide = eye[:width, :width]
    left = col_at < half

    places = [(n, u) for n in range(len(order)) for u in range(PER_SLOT)]
    for start in range(0, len(places), HEAD_GROUP):
        chains = []
        for s in places[start : start + HEAD_GROUP]:
            h = head_of(exchange, order[s[0]], s[1])
            keys = [k_heads[h, i] for i in range(2)]
            values = [v_heads[h, i] for i in range(2)]
            run_row = [row_ref[i, pl.ds(h, 1), :] for i in range(2)]
            beta_row = [row_ref[2 + i, pl.ds(h, 1), :] for i in range(2)]
            run_col = [column(x) for x in run_row]
            beta_col = [column(x) for x in beta_row]
            last_row = row_ref[4, pl.ds(h, 1), :]
            grams = [dot_nt(x, x) for x in keys]
            inv_row = [lax.rsqrt(jnp.sum(g * eye, 0, keepdims=True) + 1e-06) for g in grams]
            inv_col = [lax.rsqrt(jnp.sum(g * eye, 1, keepdims=True) + 1e-06) for g in grams]
            lowers, inverses = [], []
            for i in range(2):
                spread = jnp.exp(jnp.where(below, run_col[i] - run_row[i], 0.0))
                scaled = grams[i] * inv_row[i] * inv_col[i]
                lower = jnp.where(below, beta_col[i] * spread * scaled, 0.0)
                pair = jnp.where(apart == 1, lower, 0.0)
                step = jnp.where((apart >= 2) & (apart < 4), lower, 0.0)
                by_row = jnp.sum(pair, 1, keepdims=True)
                by_col = jnp.sum(pair, 0, keepdims=True)
                step = jnp.concatenate(
                    [step[:half], step[half:] - by_row[half:] * step[:half]], 0
                )
                swapped = jnp.concatenate([step[:, half:], step[:, :half]], 1)
                step = step - jnp.where(left, swapped * by_col, 0.0)
                lowers.append(lower)
                inverses.append(eye - pair - step)
            cross = dot_nt(keys[1], keys[0]) * inv_row[0] * inv_col[1]
            cross = cross * beta_col[1] * jnp.exp(run_col[1] - run_row[0])
            chains.append(
                dict(
                    s=s, keys=keys, values=values, run_row=run_row, beta_row=beta_row,
                    run_col=run_col, last_row=last_row, inv_row=inv_row, inv_col=inv_col,
                    lowers=lowers, inverses=inverses, cross=cross,
                )
            )
        size = 4
        while size < span:
            for c in chains:
                c["parts"] = [split(x) for x in c["inverses"]]
                c["middle"] = [
                    dot_wide(
                        split(jnp.where((apart >= size) & (apart < 2 * size), low, 0.0)), part
                    )
                    for low, part in zip(c["lowers"], c["parts"])
                ]
            for c in chains:
                c["inverses"] = [
                    x - dot_wide(part, split(mid))
                    for x, part, mid in zip(c["inverses"], c["parts"], c["middle"])
                ]
            size *= 2
        for c in chains:
            c["parts"] = [split(x) for x in c["inverses"]]
            c["middle"] = dot_wide(split(c["cross"]), c["parts"][0])
        for c in chains:
            c["corner"] = -dot_wide(c["parts"][1], split(c["middle"]))
        for c in chains:
            scale_v = c["beta_row"]
            scale_k = [
                b * jnp.exp(r) * n for b, r, n in zip(c["beta_row"], c["run_row"], c["inv_row"])
            ]
            solved = []
            for scale, source in ((scale_k, c["keys"]), (scale_v, c["values"])):
                first = split(c["inverses"][0] * scale[0])
                upper = dot(jnp.concatenate(first, 1), jnp.concatenate([source[0]] * 2, 0))
                corner = split(c["corner"] * scale[0])
                second = split(c["inverses"][1] * scale[1])
                both = jnp.concatenate(source, 0)
                lower = dot(jnp.concatenate([corner[0], second[0]], 1), both) + dot(
                    jnp.concatenate([corner[1], second[1]], 1), both
                )
                solved.append((upper, lower))
            rows = [jnp.concatenate([solved[0][i], solved[1][i]], 1) for i in range(2)]
            c["rows"] = rows
            for i in range(2):
                at = PER_SLOT * c["s"][0] + c["s"][1]
                sol_ref[at, i * span : (i + 1) * span, :] = rows[i]
        for c in chains:
            last_col = column(c["last_row"])
            weighted = []
            for i in range(2):
                remain = jnp.exp(last_col - c["run_col"][i]) * c["inv_col"][i]
                weighted.append(c["rows"][i] * jnp.concatenate([remain, remain], 1))
            high, low = split(jnp.concatenate(weighted, 0))
            keys = jnp.concatenate(c["keys"], 0)
            ends = dot_tn(keys, high) + dot_tn(keys, low)
            gate = jnp.exp(c["last_row"])
            trans = eye_wide * gate - ends[:, :width]
            slot, u = c["s"]
            out_refs[slot][u] = jnp.concatenate([trans, ends[:, width:]], 1).astype(BF16)


def stacked_beta(beta_ref, half):
    first, second = beta_ref[0], beta_ref[1]
    return [
        jnp.concatenate(
            [first[:, i * half : (i + 1) * half], second[:, i * half : (i + 1) * half]], 1
        )
        for i in range(2)
    ]


def mixing_kernel(exchange, orders, q_ref, k_heads, row_ref, *refs):
    sol_refs, (out_ref, q_all) = refs[: len(orders)], refs[len(orders) :]
    tokens, heads, width = q_ref.shape
    half = tokens // 2
    span = 2 * half
    q_all[...] = q_ref[...].astype(F32).reshape(tokens * heads, width)
    token_at = lax.broadcasted_iota(jnp.int32, (tokens, 2 * span), 0)
    row_at = lax.broadcasted_iota(jnp.int32, (tokens, 2 * span), 1)
    seen = (row_at // span) * half + lax.rem(row_at, half) <= token_at
    row_at = lax.broadcasted_iota(jnp.int32, (span, span), 0)
    col_at = lax.broadcasted_iota(jnp.int32, (span, span), 1)
    eye = (row_at == col_at).astype(F32)

    def one_head(sol_ref, s, at, h):
        queries = head_rows(q_all, h, heads)
        keys = [k_heads[h, i] for i in range(2)]
        run_col = column(row_ref[5, pl.ds(h, 1), :])
        run_row = jnp.concatenate([row_ref[i, pl.ds(h, 1), :] for i in range(2)], 1)
        inv_row = [
            lax.rsqrt(jnp.sum(dot_nt(x, x) * eye, 0, keepdims=True) + 1e-06) for x in keys
        ]
        inv_q = lax.rsqrt(jnp.sum(queries * queries, 1, keepdims=True) + 1e-06)
        inner = dot_nt(queries.astype(BF16), jnp.concatenate(keys, 0))
        spread = jnp.concatenate([run_col, run_col], 1) - run_row
        mixing = inner * inv_q * jnp.concatenate(inv_row, 1)
        mixing = jnp.where(seen, jnp.exp(jnp.where(seen, spread, 0.0)) * mixing, 0.0)
        mix_high, mix_low = split(mixing)
        sol_high, sol_low = split(sol_ref[s])
        mixed = dot(mix_high, sol_high) + dot(mix_low, sol_high) + dot(mix_high, sol_low)
        tilde = jnp.exp(run_col) * (queries * inv_q) - mixed[:, :width]
        out_ref[at] = jnp.concatenate([tilde, mixed[:, width:]], 1)

    at = 0
    for order, sol_ref in zip(orders, sol_refs):
        for n, slot in enumerate(order):
            for u in range(PER_SLOT):
                one_head(sol_ref, PER_SLOT * n + u, at, head_of(exchange, slot, u))
                at += 1


def chain_kernel(group, *refs):
    term_refs, (local_ref, prefix_ref, end_ref) = refs[:group], refs[group : group + 3]
    held = refs[group + 3]
    width = term_refs[0].shape[1]
    me = lax.rem(lax.axis_index("seq"), group)
    for s in range(group):
        held[s] = term_refs[s][...]
    for u in range(PER_SLOT):
        first = held[me, u]
        state = first[:, width:].astype(F32)
        prefix = first[:, :width].astype(F32)
        for k in range(1, group):
            local_ref[k - 1, u] = state
            prefix_ref[k - 1, u] = prefix
            block = held[me ^ k, u]
            both = dot(block[:, :width], jnp.concatenate([*split(state), *split(prefix)], 1))
            state = both[:, :width] + both[:, width : 2 * width] + block[:, width:].astype(F32)
            prefix = both[:, 2 * width : 3 * width] + both[:, 3 * width :]
        end_ref[u] = state.astype(BF16)


def entry_kernel(group, local_ref, prefix_ref, before_ref, *refs):
    out_refs, held = refs[:group], refs[group]
    me = lax.rem(lax.axis_index("seq"), group)
    for u in range(PER_SLOT):
        before = before_ref[u]
        held[0, u] = before
        for k in range(1, group):
            high, low = split(prefix_ref[k - 1, u])
            state = dot(
                jnp.concatenate([high, low], 1), jnp.concatenate([before, before], 0)
            ) + local_ref[k - 1, u]
            held[k, u] = state.astype(BF16)
    for s in range(group):
        out_refs[s][...] = held[me ^ s]


def emit_kernel(exchange, order, mixed_ref, gain_ref, residual_ref, *refs):
    width = mixed_ref.shape[2] // 2
    state_refs, out_ref = refs[: len(order)], refs[len(order)]
    for n, slot in enumerate(order):
        for u in range(PER_SLOT):
            h = head_of(exchange, slot, u)
            mixed = mixed_ref[PER_SLOT * n + u]
            state = state_refs[slot][u]
            out = dot(
                jnp.concatenate(split(mixed[:, :width]), 1), jnp.concatenate([state, state], 0)
            ) + mixed[:, width:]
            scale = lax.rsqrt(jnp.mean(out * out, 1, keepdims=True) + 1e-05)
            out = out * scale * gain_ref[...]
            columns = pl.ds(pl.multiple_of(h * width, width), width)
            out_ref[h] = (residual_ref[:, columns].astype(F32) + out).astype(BF16)


def ffn_kernel(count, gain_ref, up_at, down_at, up_ref, down_ref, *refs):
    parts, outs = refs[:count], refs[count : 2 * count]
    tiles_in, act, total = refs[2 * count :]
    groups, kept, side, _ = up_ref.shape
    tiles, tokens, _ = tiles_in.shape
    each = tiles // count
    me = lax.axis_index("tensor")
    squares = jnp.zeros((tokens, side), F32)
    for part in parts:
        for b in range(each):
            wide = part[b].astype(F32)
            squares += wide * wide
    scale = lax.rsqrt(jnp.sum(squares, 1, keepdims=True) / (tiles * side) + 1e-05)
    for m, part in enumerate(parts):
        base = (me ^ m) * each
        for b in range(each):
            gain = gain_ref[pl.ds(base + b, 1), :]
            tiles_in[base + b] = (part[b].astype(F32) * scale * gain).astype(BF16)
    for c in range(groups):
        picked = jnp.concatenate([tiles_in[up_at[c, j]] for j in range(kept)], 1)
        pre = dot(picked, up_ref[c].reshape(kept * side, side))
        act[c] = jax.nn.gelu(pre).astype(BF16)
    total[...] = jnp.zeros_like(total)
    for c in range(groups):
        now = act[c]
        for j in range(0, kept, 2):
            both = dot(now, jnp.concatenate([down_ref[c, j], down_ref[c, j + 1]], 1))
            total[down_at[c, j]] += both[:, :side]
            total[down_at[c, j + 1]] += both[:, side:]
    for m, out in enumerate(outs):
        base = (me ^ m) * each
        out[...] = total[pl.ds(base, each)].astype(BF16)


def final_kernel(hidden_ref, *refs):
    out_ref = refs[-1]
    tiles, _, side = hidden_ref.shape
    for b in range(tiles):
        total = refs[0][b].astype(F32)
        for ref in refs[1:-1]:
            total += ref[b].astype(F32)
        out_ref[:, b * side : (b + 1) * side] = (hidden_ref[b].astype(F32) + total).astype(BF16)


def local_call(kernel, out_shape, ins, args, scratch=(), flops=0, moved=0, limit=20 * MIB):
    return pl.pallas_call(
        kernel,
        out_shape=out_shape,
        in_specs=ins,
        out_specs=jax.tree.map(lambda _: VMEM, out_shape),
        scratch_shapes=scratch,
        compiler_params=pltpu.CompilerParams(vmem_limit_bytes=limit),
        cost_estimate=pl.CostEstimate(flops=flops, bytes_accessed=moved, transcendentals=0),
    )(*args)


def prefix_states(terms):
    count, index = lax.axis_size("seq"), lax.axis_index("seq")
    own = jnp.stack([terms[s] for s in sorted(terms)])
    everything = lax.all_gather(own, "seq")
    width = own.shape[2]

    def step(k, state):
        block = everything[k]
        new = jnp.einsum(
            "sude,suef->sudf",
            block[..., :width].astype(F32),
            state,
            precision=lax.Precision.HIGHEST,
        ) + block[..., width:].astype(F32)
        return jnp.where(k < index, new, state)

    start = jnp.zeros((*own.shape[:3], width), F32)
    states = lax.fori_loop(0, count, step, start).astype(BF16)
    return {s: states[s] for s in range(len(terms))}


def per_device(
    queries, keys, values, beta, decay, out_gain, residual, ffn_gain,
    up_blocks, up_index, down_kept_tiles, down_index,
):
    tokens, heads, width = queries.shape
    seq_count, tensor_count = lax.axis_size("seq"), lax.axis_size("tensor")
    slots = heads // PER_SLOT
    exchange = slots if seq_count == 2 * slots and slots & (slots - 1) == 0 else 0
    order = sorted(range(slots), key=lambda s: -(s & 1) * slots - s)
    cuts = [0, *(n for n in CUTS if n < slots), slots]
    orders = [order[n:m] for n, m in zip(cuts, cuts[1:])]
    swaps = [[(k, k ^ s) for k in range(seq_count)] for s in range(slots)]
    term = jax.ShapeDtypeStruct((PER_SLOT, width, 2 * width), BF16)
    by_head = jax.ShapeDtypeStruct((heads, 2, tokens, width), BF16)
    rows = jax.ShapeDtypeStruct((6, heads, tokens), F32)
    terms, solved, arrived = {}, [], {}
    for part in orders:
        solution_rows = jax.ShapeDtypeStruct(
            (PER_SLOT * len(part), 2 * tokens, 2 * width), F32
        )
        outs = [term] * len(part) + [solution_rows]
        if not terms:
            *given, sol, k_heads, v_heads, row_terms = local_call(
                functools.partial(first_kernel, exchange, part),
                outs + [by_head, by_head, rows],
                [ANY] * 4,
                (beta, decay, keys, values),
                [
                    pltpu.VMEM(beta.shape, F32),
                    pltpu.VMEM(decay.shape, F32),
                    pltpu.VMEM(keys.shape, BF16),
                    pltpu.VMEM(values.shape, BF16),
                    pltpu.VMEM((2, tokens * heads, width), F32),
                    pltpu.VMEM((2, tokens * heads, width), F32),
                    pltpu.SemaphoreType.DMA((4,)),
                ],
                limit=FIRST_LIMIT,
            )
        else:
            *given, sol = local_call(
                functools.partial(later_kernel, exchange, part),
                outs,
                [VMEM] * 3,
                (k_heads, v_heads, row_terms),
            )
        terms.update(zip(part, given))
        solved.append(sol)
        if exchange:
            for s in part:
                arrived[s] = lax.ppermute(terms[s], "seq", swaps[s]) if s else terms[s]
    mixed = local_call(
        functools.partial(mixing_kernel, exchange, orders),
        jax.ShapeDtypeStruct((heads, tokens, 2 * width), F32),
        [VMEM] * (3 + len(orders)),
        (queries, k_heads, row_terms, *solved),
        [pltpu.VMEM((tokens * heads, width), F32)],
        flops=3_000_000_000,
    )
    state = jax.ShapeDtypeStruct((PER_SLOT, width, width), BF16)
    if exchange:
        inner = jax.ShapeDtypeStruct((slots - 1, PER_SLOT, width, width), F32)
        local, prefix, end = local_call(
            functools.partial(chain_kernel, slots),
            [inner, inner, state],
            [VMEM] * slots,
            [arrived[s] for s in range(slots)],
            [pltpu.VMEM((slots, PER_SLOT, width, 2 * width), BF16)],
        )
        before = lax.ppermute(end, "seq", [(k, k + slots) for k in range(slots)])
        outgoing = local_call(
            functools.partial(entry_kernel, slots),
            [state] * slots,
            [VMEM] * 3,
            (local, prefix, before),
            [pltpu.VMEM((slots, PER_SLOT, width, width), BF16)],
        )
        states = {0: outgoing[0]}
        for s in order[:-1]:
            states[s] = lax.ppermute(outgoing[s], "seq", swaps[s])
    else:
        states = prefix_states(terms)
    hidden = local_call(
        functools.partial(emit_kernel, exchange, order),
        jax.ShapeDtypeStruct((heads, tokens, width), BF16),
        [VMEM] * (3 + slots),
        (mixed, out_gain.reshape(1, width), residual, *(states[s] for s in range(slots))),
    )

    flips = {
        d: [(k, k ^ d) for k in range(tensor_count)]
        for d in (1 << b for b in range(tensor_count.bit_length() - 1))
    }
    parts = {0: hidden}
    for d in sorted(flips, reverse=True):
        for m in list(parts):
            parts[m | d] = lax.ppermute(parts[m], "tensor", flips[d])
    groups, kept, side, _ = up_blocks.shape
    tiles = heads * tensor_count
    sums = local_call(
        functools.partial(ffn_kernel, tensor_count),
        [jax.ShapeDtypeStruct((heads, tokens, side), BF16)] * tensor_count,
        [VMEM, SMEM, SMEM, VMEM, VMEM] + [VMEM] * tensor_count,
        (
            ffn_gain.reshape(tiles, side), up_index, down_index, up_blocks, down_kept_tiles,
            *(parts[m] for m in range(tensor_count)),
        ),
        [
            pltpu.VMEM((tiles, tokens, side), BF16),
            pltpu.VMEM((groups, tokens, side), BF16),
            pltpu.VMEM((tiles, tokens, side), F32),
        ],
    )
    held = {m: [part] for m, part in enumerate(sums)}
    for d in sorted(flips):
        for m in [m for m in held if not m & d]:
            moved = lax.ppermute(added(held.pop(m | d)), "tensor", flips[d])
            held[m].append(moved)
    return local_call(
        final_kernel,
        jax.ShapeDtypeStruct((tokens, heads * side), BF16),
        [VMEM] * (1 + len(held[0])),
        (hidden, *held[0]),
    )


def added(terms):
    if len(terms) == 1:
        return terms[0]
    return sum(term.astype(F32) for term in terms).astype(BF16)


def solution(mesh):
    placed = (
        P("seq", "tensor", None),
        P(None, "seq", "tensor", None),
        P(None, "seq", "tensor", None),
        P(None, "tensor", "seq"),
        P("tensor", "seq"),
        P(),
        P("seq", "tensor"),
        P(),
        P("tensor", None, None, None),
        P("tensor", None),
        P("tensor", None, None, None),
        P("tensor", None),
    )
    return jax.shard_map(
        per_device, mesh=mesh, in_specs=placed, out_specs=P("seq", "tensor"), check_vma=False
    )
```

```python
import functools

import jax
import jax.numpy as jnp
from jax import lax
from jax.experimental import pallas as pl
from jax.experimental.pallas import tpu as pltpu
from jax.sharding import PartitionSpec as P

F32 = jnp.float32
BF16 = jnp.bfloat16
HEAD_GROUP = 6
PER_SLOT = 2
CUTS = (1, 3)
PIECES = [[0, 1, 2, 3]]
FIRST_LIMIT = 52 * (1 << 20) + (1 << 19)
MIB = 1 << 20
VMEM = pl.BlockSpec(memory_space=pltpu.VMEM)
SMEM = pl.BlockSpec(memory_space=pltpu.SMEM)
ANY = pl.BlockSpec(memory_space=pl.ANY)


def dot(a, b):
    return jnp.dot(a, b, preferred_element_type=F32)


def dot_nt(a, b):
    return lax.dot_general(a, b, (((1,), (1,)), ((), ())), preferred_element_type=F32)


def dot_tn(a, b):
    return lax.dot_general(a, b, (((0,), (0,)), ((), ())), preferred_element_type=F32)


def split(x):
    high = x.astype(BF16)
    return high, (x - high.astype(F32)).astype(BF16)


def dot_wide(a, b):
    width = a[0].shape[1]
    row = jnp.concatenate([b[0], b[1]], 1)
    out = dot(jnp.concatenate([a[0], a[1]], 1), jnp.concatenate([row, row], 0))
    return out[:, :width] + out[:, width:]


def column(row):
    n = row.shape[1]
    return jnp.broadcast_to(row, (n, n)).T


def head_rows(ref, h, stride):
    return ref[pl.ds(h, ref.shape[0] // stride, stride=stride), :]


def stacked(first, second):
    half = first.shape[0] // 2
    return [
        jnp.concatenate([first[i * half : (i + 1) * half], second[i * half : (i + 1) * half]], 0)
        for i in range(2)
    ]


def running_rows(decay_ref):
    tokens = decay_ref.shape[1]
    earlier = lax.broadcasted_iota(jnp.int32, (tokens, tokens), 0)
    later = lax.broadcasted_iota(jnp.int32, (tokens, tokens), 1)
    return jnp.dot(
        decay_ref[...],
        (earlier <= later).astype(F32),
        preferred_element_type=F32,
        precision=lax.Precision.HIGHEST,
    )


def doubled(rows, half):
    return [
        jnp.concatenate([rows[:, i * half : (i + 1) * half]] * 2, 1) for i in range(2)
    ]


def head_of(exchange, slot, u):
    if exchange:
        return PER_SLOT * (lax.rem(lax.axis_index("seq"), exchange) ^ slot) + u
    return PER_SLOT * slot + u


def sort_kernel(k_hbm, v_hbm, k_heads, v_heads, k_ref, v_ref, wide, sems):
    _, tokens, heads, width = k_hbm.shape
    copies = [
        pltpu.make_async_copy(source, target, sems.at[n])
        for n, (source, target) in enumerate(((k_hbm, k_ref), (v_hbm, v_ref)))
    ]
    for copy in copies:
        copy.start()
    for n, (source, target) in enumerate(((k_ref, k_heads), (v_ref, v_heads))):
        copies[n].wait()
        for j in range(2):
            wide[n, j] = source[j].astype(F32).reshape(tokens * heads, width)
        for h in range(heads):
            rows = stacked(*(head_rows(wide.at[n, j], h, heads) for j in range(2)))
            for i in range(2):
                target[h, i] = rows[i].astype(BF16)


def first_kernel(exchange, order, given_ref, k_heads, v_heads, *refs):
    _, heads, tokens = given_ref.shape
    beta_ref, decay_ref = given_ref.at[:2], given_ref.at[2]
    half = tokens // 2
    out_refs, (sol_ref, row_ref) = refs[: len(order)], refs[len(order) :]
    run = running_rows(decay_ref)
    run_half = doubled(run, half)
    beta_half = stacked_beta(beta_ref, half)
    for i in range(2):
        row_ref[i] = run_half[i]
        row_ref[2 + i] = beta_half[i]
    row_ref[4] = jnp.broadcast_to(run[:, tokens - 1 :], (heads, 2 * half))
    row_ref[5] = run
    solve_heads(exchange, order, k_heads, v_heads, row_ref, out_refs, sol_ref)


def later_kernel(exchange, order, k_heads, v_heads, row_ref, *refs):
    *out_refs, sol_ref = refs[-1 - len(order) :]
    solve_heads(exchange, order, k_heads, v_heads, row_ref, out_refs, sol_ref)


def solve_heads(exchange, order, k_heads, v_heads, row_ref, out_refs, sol_ref):
    span, width = k_heads.shape[2:]
    half = span // 2
    row_at = lax.broadcasted_iota(jnp.int32, (span, span), 0)
    col_at = lax.broadcasted_iota(jnp.int32, (span, span), 1)
    row_time = 2 * lax.rem(row_at, half) + row_at // half
    col_time = 2 * lax.rem(col_at, half) + col_at // half
    below = col_time < row_time
    apart = jnp.where(below, row_time ^ col_time, 0)
    eye = (row_at == col_at).astype(F32)
    eye_wide = eye[:width, :width]
    left = col_at < half

    places = [(n, u) for n in range(len(order)) for u in range(PER_SLOT)]
    for start in range(0, len(places), HEAD_GROUP):
        chains = []
        for s in places[start : start + HEAD_GROUP]:
            h = head_of(exchange, order[s[0]], s[1])
            keys = [k_heads[h, i] for i in range(2)]
            run_row = [row_ref[i, pl.ds(h, 1), :] for i in range(2)]
            beta_row = [row_ref[2 + i, pl.ds(h, 1), :] for i in range(2)]
            run_col = [column(x) for x in run_row]
            beta_col = [column(x) for x in beta_row]
            last_row = row_ref[4, pl.ds(h, 1), :]
            grams = [dot_nt(x, x) for x in keys]
            inv_row = [lax.rsqrt(jnp.sum(g * eye, 0, keepdims=True) + 1e-06) for g in grams]
            inv_col = [lax.rsqrt(jnp.sum(g * eye, 1, keepdims=True) + 1e-06) for g in grams]
            lowers, inverses = [], []
            for i in range(2):
                spread = jnp.exp(jnp.where(below, run_col[i] - run_row[i], 0.0))
                scaled = grams[i] * inv_row[i] * inv_col[i]
                lower = jnp.where(below, beta_col[i] * spread * scaled, 0.0)
                pair = jnp.where(apart == 1, lower, 0.0)
                step = jnp.where((apart >= 2) & (apart < 4), lower, 0.0)
                by_row = jnp.sum(pair, 1, keepdims=True)
                by_col = jnp.sum(pair, 0, keepdims=True)
                step = jnp.concatenate(
                    [step[:half], step[half:] - by_row[half:] * step[:half]], 0
                )
                swapped = jnp.concatenate([step[:, half:], step[:, :half]], 1)
                step = step - jnp.where(left, swapped * by_col, 0.0)
                lowers.append(lower)
                inverses.append(eye - pair - step)
            cross = dot_nt(keys[1], keys[0]) * inv_row[0] * inv_col[1]
            cross = cross * beta_col[1] * jnp.exp(run_col[1] - run_row[0])
            chains.append(
                dict(
                    s=s, h=h, keys=keys, run_row=run_row, beta_row=beta_row,
                    run_col=run_col, last_row=last_row, inv_row=inv_row, inv_col=inv_col,
                    lowers=lowers, inverses=inverses, cross=cross,
                )
            )
        size = 4
        while size < span:
            top = min(4 * size, span)
            for c in chains:
                c["parts"] = [split(x) for x in c["inverses"]]
                c["steps"] = [
                    split(
                        dot_wide(
                            part, split(jnp.where((apart >= size) & (apart < top), low, 0.0))
                        )
                    )
                    for low, part in zip(c["lowers"], c["parts"])
                ]
            for c in chains:
                c["inverses"] = [
                    x - dot_wide(step, part)
                    for x, step, part in zip(c["inverses"], c["steps"], c["parts"])
                ]
            if top == 4 * size:
                for c in chains:
                    c["steps"] = [split(dot_wide(step, step)) for step in c["steps"]]
                for c in chains:
                    c["inverses"] = [
                        x + dot_wide(step, split(x)) for x, step in zip(c["inverses"], c["steps"])
                    ]
            size = top
        for c in chains:
            c["parts"] = [split(x) for x in c["inverses"]]
            c["middle"] = dot_wide(split(c["cross"]), c["parts"][0])
        for c in chains:
            c["corner"] = -dot_wide(c["parts"][1], split(c["middle"]))
        for c in chains:
            values = [v_heads[c["h"], i] for i in range(2)]
            scale_v = c["beta_row"]
            scale_k = [
                b * jnp.exp(r) * n for b, r, n in zip(c["beta_row"], c["run_row"], c["inv_row"])
            ]
            solved = []
            for scale, source in ((scale_k, c["keys"]), (scale_v, values)):
                first = split(c["inverses"][0] * scale[0])
                upper = dot(jnp.concatenate(first, 1), jnp.concatenate([source[0]] * 2, 0))
                corner = split(c["corner"] * scale[0])
                second = split(c["inverses"][1] * scale[1])
                both = jnp.concatenate(source, 0)
                lower = dot(jnp.concatenate([corner[0], second[0]], 1), both) + dot(
                    jnp.concatenate([corner[1], second[1]], 1), both
                )
                solved.append((upper, lower))
            rows = [jnp.concatenate([solved[0][i], solved[1][i]], 1) for i in range(2)]
            c["rows"] = rows
            for i in range(2):
                at = PER_SLOT * c["s"][0] + c["s"][1]
                sol_ref[at, i * span : (i + 1) * span, :] = rows[i]
        for c in chains:
            last_col = column(c["last_row"])
            weighted = []
            for i in range(2):
                remain = jnp.exp(last_col - c["run_col"][i]) * c["inv_col"][i]
                weighted.append(c["rows"][i] * jnp.concatenate([remain, remain], 1))
            high, low = split(jnp.concatenate(weighted, 0))
            keys = jnp.concatenate(c["keys"], 0)
            ends = dot_tn(keys, high) + dot_tn(keys, low)
            gate = jnp.exp(c["last_row"])
            trans = eye_wide * gate - ends[:, :width]
            slot, u = c["s"]
            out_refs[slot][u] = jnp.concatenate([trans, ends[:, width:]], 1).astype(BF16)


def stacked_beta(beta_ref, half):
    first, second = beta_ref[0], beta_ref[1]
    return [
        jnp.concatenate(
            [first[:, i * half : (i + 1) * half], second[:, i * half : (i + 1) * half]], 1
        )
        for i in range(2)
    ]


def queries_kernel(q_ref, *refs):
    out_ref, q_all = refs[-2:]
    tokens, heads, width = q_ref.shape
    q_all[...] = q_ref[...].astype(F32).reshape(tokens * heads, width)
    for h in range(heads):
        out_ref[h] = head_rows(q_all, h, heads).astype(BF16)


def mixing_kernel(exchange, orders, q_heads, k_heads, row_ref, *refs):
    sol_refs, out_ref = refs[: len(orders)], refs[-1]
    heads, tokens, width = q_heads.shape
    half = tokens // 2
    span = 2 * half
    token_at = lax.broadcasted_iota(jnp.int32, (tokens, 2 * span), 0)
    row_at = lax.broadcasted_iota(jnp.int32, (tokens, 2 * span), 1)
    seen = (row_at // span) * half + lax.rem(row_at, half) <= token_at
    row_at = lax.broadcasted_iota(jnp.int32, (span, span), 0)
    col_at = lax.broadcasted_iota(jnp.int32, (span, span), 1)
    eye = (row_at == col_at).astype(F32)

    def one_head(sol_ref, s, at, h):
        queries = q_heads[h].astype(F32)
        keys = [k_heads[h, i] for i in range(2)]
        run_col = column(row_ref[5, pl.ds(h, 1), :])
        run_row = jnp.concatenate([row_ref[i, pl.ds(h, 1), :] for i in range(2)], 1)
        inv_row = [
            lax.rsqrt(jnp.sum(dot_nt(x, x) * eye, 0, keepdims=True) + 1e-06) for x in keys
        ]
        inv_q = lax.rsqrt(jnp.sum(queries * queries, 1, keepdims=True) + 1e-06)
        inner = dot_nt(queries.astype(BF16), jnp.concatenate(keys, 0))
        spread = jnp.concatenate([run_col, run_col], 1) - run_row
        mixing = inner * inv_q * jnp.concatenate(inv_row, 1)
        mixing = jnp.where(seen, jnp.exp(jnp.where(seen, spread, 0.0)) * mixing, 0.0)
        mix_high, mix_low = split(mixing)
        sol_high, sol_low = split(sol_ref[s])
        mixed = dot(mix_high, sol_high) + dot(mix_low, sol_high) + dot(mix_high, sol_low)
        tilde = jnp.exp(run_col) * (queries * inv_q) - mixed[:, :width]
        out_ref[at] = jnp.concatenate([tilde, mixed[:, width:]], 1)

    at = 0
    for order, sol_ref in zip(orders, sol_refs):
        for n, slot in enumerate(order):
            for u in range(PER_SLOT):
                one_head(sol_ref, PER_SLOT * n + u, at, head_of(exchange, slot, u))
                at += 1


def chain_kernel(order, *refs):
    group = len(order)
    term_refs, (local_ref, prefix_ref, end_ref) = refs[:group], refs[group : group + 3]
    held = refs[group + 3]
    width = term_refs[0].shape[1]
    me = lax.rem(lax.axis_index("seq"), group)
    for n, s in enumerate(order):
        held[s] = term_refs[n][...]
    for u in range(PER_SLOT):
        first = held[me, u]
        state = first[:, width:].astype(F32)
        prefix = first[:, :width].astype(F32)
        for k in range(1, group):
            local_ref[k - 1, u] = state
            prefix_ref[k - 1, u] = prefix
            block = held[me ^ k, u]
            both = dot(block[:, :width], jnp.concatenate([*split(state), *split(prefix)], 1))
            state = both[:, :width] + both[:, width : 2 * width] + block[:, width:].astype(F32)
            prefix = both[:, 2 * width : 3 * width] + both[:, 3 * width :]
        end_ref[u] = state.astype(BF16)


def entry_kernel(group, local_ref, prefix_ref, before_ref, *refs):
    out_refs, held = refs[:group], refs[group]
    me = lax.rem(lax.axis_index("seq"), group)
    for u in range(PER_SLOT):
        before = before_ref[u]
        held[0, u] = before
        for k in range(1, group):
            high, low = split(prefix_ref[k - 1, u])
            state = dot(
                jnp.concatenate([high, low], 1), jnp.concatenate([before, before], 0)
            ) + local_ref[k - 1, u]
            held[k, u] = state.astype(BF16)
    for s in range(group):
        out_refs[s][...] = held[me ^ s]


def emit_kernel(exchange, order, slots, mixed_ref, gain_ref, residual_ref, *refs):
    width = mixed_ref.shape[2] // 2
    state_refs, out_ref = refs[: len(slots)], refs[len(slots)]
    for n, slot in enumerate(slots):
        for u in range(PER_SLOT):
            h = head_of(exchange, slot, u)
            mixed = mixed_ref[PER_SLOT * order.index(slot) + u]
            state = state_refs[n][u]
            out = dot(
                jnp.concatenate(split(mixed[:, :width]), 1), jnp.concatenate([state, state], 0)
            ) + mixed[:, width:]
            scale = lax.rsqrt(jnp.mean(out * out, 1, keepdims=True) + 1e-05)
            out = out * scale * gain_ref[...]
            columns = pl.ds(pl.multiple_of(h * width, width), width)
            out_ref[PER_SLOT * n + u] = (
                residual_ref[:, columns].astype(F32) + out
            ).astype(BF16)


def ffn_kernel(count, exchange, pieces, gain_ref, up_at, down_at, up_ref, down_ref, *refs):
    given, outs = refs[: count * len(pieces)], refs[count * len(pieces) :][:count]
    tiles_in, act, total = refs[count * (len(pieces) + 1) :]
    groups, kept, side, _ = up_ref.shape
    tiles, tokens, _ = tiles_in.shape
    each = tiles // count
    me = lax.axis_index("tensor")
    squares = jnp.zeros((tokens, side), F32)
    for n, part in enumerate(given):
        base = (me ^ (n // len(pieces))) * each
        for i, slot in enumerate(pieces[n % len(pieces)]):
            for u in range(PER_SLOT):
                tile = base + head_of(exchange, slot, u)
                wide = part[PER_SLOT * i + u].astype(F32)
                squares += wide * wide
                tiles_in[tile] = (wide * gain_ref[pl.ds(tile, 1), :]).astype(BF16)
    scale = lax.rsqrt(jnp.sum(squares, 1, keepdims=True) / (tiles * side) + 1e-05)
    scale = jnp.broadcast_to(scale, (tokens, side))
    for c in range(groups):
        picked = jnp.concatenate([tiles_in[up_at[c, j]] for j in range(kept)], 1)
        pre = dot(picked, up_ref[c].reshape(kept * side, side))
        act[c] = jax.nn.gelu(pre * scale).astype(BF16)
    total[...] = jnp.zeros_like(total)
    for c in range(groups):
        now = act[c]
        for j in range(0, kept, 2):
            both = dot(now, jnp.concatenate([down_ref[c, j], down_ref[c, j + 1]], 1))
            total[down_at[c, j]] += both[:, :side]
            total[down_at[c, j + 1]] += both[:, side:]
    for m, out in enumerate(outs):
        base = (me ^ m) * each
        out[...] = total[pl.ds(base, each)].astype(BF16)


def final_kernel(exchange, pieces, *refs):
    given, sums, out_ref = refs[: len(pieces)], refs[len(pieces) : -1], refs[-1]
    side = given[0].shape[2]
    for part, slots in zip(given, pieces):
        for i, slot in enumerate(slots):
            for u in range(PER_SLOT):
                tile = head_of(exchange, slot, u)
                total = sums[0][tile].astype(F32)
                for ref in sums[1:]:
                    total += ref[tile].astype(F32)
                columns = pl.ds(pl.multiple_of(tile * side, side), side)
                out_ref[:, columns] = (
                    part[PER_SLOT * i + u].astype(F32) + total
                ).astype(BF16)


def local_call(kernel, out_shape, ins, args, scratch=(), flops=0, moved=0, limit=8 * MIB):
    return pl.pallas_call(
        kernel,
        out_shape=out_shape,
        in_specs=ins,
        out_specs=jax.tree.map(lambda _: VMEM, out_shape),
        scratch_shapes=scratch,
        compiler_params=pltpu.CompilerParams(vmem_limit_bytes=limit),
        cost_estimate=pl.CostEstimate(flops=flops, bytes_accessed=moved, transcendentals=0),
    )(*args)


def prefix_states(terms):
    count, index = lax.axis_size("seq"), lax.axis_index("seq")
    own = jnp.stack([terms[s] for s in sorted(terms)])
    everything = lax.all_gather(own, "seq")
    width = own.shape[2]

    def step(k, state):
        block = everything[k]
        new = jnp.einsum(
            "sude,suef->sudf",
            block[..., :width].astype(F32),
            state,
            precision=lax.Precision.HIGHEST,
        ) + block[..., width:].astype(F32)
        return jnp.where(k < index, new, state)

    start = jnp.zeros((*own.shape[:3], width), F32)
    states = lax.fori_loop(0, count, step, start).astype(BF16)
    return {s: states[s] for s in range(len(terms))}


def per_device(
    queries, keys, values, beta, decay, out_gain, residual, ffn_gain,
    up_blocks, up_index, down_kept_tiles, down_index,
):
    tokens, heads, width = queries.shape
    seq_count, tensor_count = lax.axis_size("seq"), lax.axis_size("tensor")
    slots = heads // PER_SLOT
    exchange = slots if seq_count == 2 * slots and slots & (slots - 1) == 0 else 0
    order = sorted(range(slots), key=lambda s: -(s & 1) * slots - s)
    cuts = [0, *(n for n in CUTS if n < slots), slots]
    orders = [order[n:m] for n, m in zip(cuts, cuts[1:])]
    swaps = [[(k, k ^ s) for k in range(seq_count)] for s in range(slots)]
    term = jax.ShapeDtypeStruct((PER_SLOT, width, 2 * width), BF16)
    by_head = jax.ShapeDtypeStruct((heads, 2, tokens, width), BF16)
    rows = jax.ShapeDtypeStruct((6, heads, tokens), F32)
    terms, solved, arrived = {}, [], {}
    for part in orders:
        solution_rows = jax.ShapeDtypeStruct(
            (PER_SLOT * len(part), 2 * tokens, 2 * width), F32
        )
        outs = [term] * len(part) + [solution_rows]
        if not terms:
            k_heads, v_heads = local_call(
                sort_kernel,
                [by_head, by_head],
                [ANY] * 2,
                (keys, values),
                [
                    pltpu.VMEM(keys.shape, BF16),
                    pltpu.VMEM(values.shape, BF16),
                    pltpu.VMEM((2, 2, tokens * heads, width), F32),
                    pltpu.SemaphoreType.DMA((2,)),
                ],
                limit=FIRST_LIMIT,
            )
            *given, sol, row_terms = local_call(
                functools.partial(first_kernel, exchange, part),
                outs + [rows],
                [VMEM] * 3,
                (jnp.concatenate([beta, decay[None]]), k_heads, v_heads),
                limit=16 * MIB,
            )
        else:
            first = [arrived[order[0]]] if part == order[-1:] and arrived else []
            *given, sol = local_call(
                functools.partial(later_kernel, exchange, part),
                outs,
                [VMEM] * 3 + [ANY] * len(first),
                (k_heads, v_heads, row_terms, *first),
                flops=0,
            )
        terms.update(zip(part, given))
        solved.append(sol)
        if exchange:
            for s in part:
                arrived[s] = lax.ppermute(terms[s], "seq", swaps[s]) if s else terms[s]
    groups, _, side, _ = up_blocks.shape
    tiles = heads * tensor_count
    state = jax.ShapeDtypeStruct((PER_SLOT, width, width), BF16)
    q_heads = local_call(
        queries_kernel,
        jax.ShapeDtypeStruct((heads, tokens, width), BF16),
        [VMEM] + [ANY] * len(orders),
        (queries, *solved),
        [pltpu.VMEM((tokens * heads, width), F32)],
        flops=3_000_000_000,
    )

    def mix(after):
        return local_call(
            functools.partial(mixing_kernel, exchange, orders),
            jax.ShapeDtypeStruct((heads, tokens, 2 * width), F32),
            [VMEM] * (3 + len(orders)) + [ANY],
            (q_heads, k_heads, row_terms, *solved, after),
            flops=3_000_000_000,
        )

    if exchange:
        late = order[-1:] + order[:-1]
        inner = jax.ShapeDtypeStruct((slots - 1, PER_SLOT, width, width), F32)
        local, prefix, end = local_call(
            functools.partial(chain_kernel, late),
            [inner, inner, state],
            [VMEM] * slots,
            [arrived[s] for s in late],
            [pltpu.VMEM((slots, PER_SLOT, width, 2 * width), BF16)],
        )
        mixed = mix(end)
        before = lax.ppermute(end, "seq", [(k, k + slots) for k in range(slots)])
        outgoing = local_call(
            functools.partial(entry_kernel, slots),
            [state] * slots,
            [VMEM] * 3,
            (local, prefix, before),
            [pltpu.VMEM((slots, PER_SLOT, width, width), BF16)],
        )
        states = {0: outgoing[0]}
        for s in order[:-1]:
            states[s] = lax.ppermute(outgoing[s], "seq", swaps[s])
    else:
        states = prefix_states(terms)
        mixed = mix(terms[0])
    pieces = PIECES if exchange and slots == 4 else [list(range(slots))]
    hidden = [
        local_call(
            functools.partial(emit_kernel, exchange, order, piece),
            jax.ShapeDtypeStruct((PER_SLOT * len(piece), tokens, width), BF16),
            [VMEM] * (3 + len(piece)),
            (mixed, out_gain.reshape(1, width), residual, *(states[s] for s in piece)),
        )
        for piece in pieces
    ]

    flips = {
        d: [(k, k ^ d) for k in range(tensor_count)]
        for d in (1 << b for b in range(tensor_count.bit_length() - 1))
    }
    parts = [{0: given} for given in hidden]
    for held in parts:
        for d in sorted(flips, reverse=True):
            for m in list(held):
                held[m | d] = lax.ppermute(held[m], "tensor", flips[d])
    sums = local_call(
        functools.partial(ffn_kernel, tensor_count, exchange, pieces),
        [jax.ShapeDtypeStruct((heads, tokens, side), BF16)] * tensor_count,
        [VMEM, SMEM, SMEM, VMEM, VMEM] + [VMEM] * (tensor_count * len(pieces)),
        (
            ffn_gain.reshape(tiles, side), up_index, down_index, up_blocks, down_kept_tiles,
            *(held[m] for m in range(tensor_count) for held in parts),
        ),
        [
            pltpu.VMEM((tiles, tokens, side), BF16),
            pltpu.VMEM((groups, tokens, side), BF16),
            pltpu.VMEM((tiles, tokens, side), F32),
        ],
        limit=20 * MIB,
    )
    held = {m: [given] for m, given in enumerate(sums)}
    for d in sorted(flips):
        for m in [m for m in held if not m & d]:
            moved = lax.ppermute(added(held.pop(m | d)), "tensor", flips[d])
            held[m].append(moved)
    moved = held[0]
    return local_call(
        functools.partial(final_kernel, exchange, pieces),
        jax.ShapeDtypeStruct((tokens, heads * side), BF16),
        [VMEM] * (len(pieces) + len(moved)),
        (*hidden, *moved),
    )


def added(terms):
    if len(terms) == 1:
        return terms[0]
    return sum(term.astype(F32) for term in terms).astype(BF16)


def solution(mesh):
    placed = (
        P("seq", "tensor", None),
        P(None, "seq", "tensor", None),
        P(None, "seq", "tensor", None),
        P(None, "tensor", "seq"),
        P("tensor", "seq"),
        P(),
        P("seq", "tensor"),
        P(),
        P("tensor", None, None, None),
        P("tensor", None),
        P("tensor", None, None, None),
        P("tensor", None),
    )
    return jax.shard_map(
        per_device, mesh=mesh, in_specs=placed, out_specs=P("seq", "tensor"), check_vma=False
    )
```

```python
import functools

import jax
import jax.numpy as jnp
from jax import lax
from jax.experimental import pallas as pl
from jax.experimental.pallas import tpu as pltpu
from jax.sharding import PartitionSpec as P

F32 = jnp.float32
BF16 = jnp.bfloat16
HEAD_GROUP = 6
PER_SLOT = 2
CUTS = (1, 3)
PIECES = [[0, 1, 2, 3]]
FIRST_LIMIT = 52 * (1 << 20) + (1 << 19)
MIB = 1 << 20
VMEM = pl.BlockSpec(memory_space=pltpu.VMEM)
SMEM = pl.BlockSpec(memory_space=pltpu.SMEM)
ANY = pl.BlockSpec(memory_space=pl.ANY)


def dot(a, b):
    return jnp.dot(a, b, preferred_element_type=F32)


def dot_nt(a, b):
    return lax.dot_general(a, b, (((1,), (1,)), ((), ())), preferred_element_type=F32)


def dot_tn(a, b):
    return lax.dot_general(a, b, (((0,), (0,)), ((), ())), preferred_element_type=F32)


def split(x):
    high = x.astype(BF16)
    return high, (x - high.astype(F32)).astype(BF16)


def dot_wide(a, b):
    width = a[0].shape[1]
    row = jnp.concatenate([b[0], b[1]], 1)
    out = dot(jnp.concatenate([a[0], a[1]], 1), jnp.concatenate([row, row], 0))
    return out[:, :width] + out[:, width:]


def column(row):
    n = row.shape[1]
    return jnp.broadcast_to(row, (n, n)).T


def head_rows(ref, h, stride):
    return ref[pl.ds(h, ref.shape[0] // stride, stride=stride), :]


def stacked(first, second):
    half = first.shape[0] // 2
    return [
        jnp.concatenate([first[i * half : (i + 1) * half], second[i * half : (i + 1) * half]], 0)
        for i in range(2)
    ]


def running_rows(decay_ref):
    tokens = decay_ref.shape[1]
    earlier = lax.broadcasted_iota(jnp.int32, (tokens, tokens), 0)
    later = lax.broadcasted_iota(jnp.int32, (tokens, tokens), 1)
    return jnp.dot(
        decay_ref[...],
        (earlier <= later).astype(F32),
        preferred_element_type=F32,
        precision=lax.Precision.HIGHEST,
    )


def doubled(rows, half):
    return [
        jnp.concatenate([rows[:, i * half : (i + 1) * half]] * 2, 1) for i in range(2)
    ]


def head_of(exchange, slot, u):
    if exchange:
        return PER_SLOT * (lax.rem(lax.axis_index("seq"), exchange) ^ slot) + u
    return PER_SLOT * slot + u


def sort_kernel(k_hbm, v_hbm, k_heads, v_heads, k_ref, v_ref, wide, sems):
    _, tokens, heads, width = k_hbm.shape
    copies = [
        pltpu.make_async_copy(source, target, sems.at[n])
        for n, (source, target) in enumerate(((k_hbm, k_ref), (v_hbm, v_ref)))
    ]
    for copy in copies:
        copy.start()
    for n, (source, target) in enumerate(((k_ref, k_heads), (v_ref, v_heads))):
        copies[n].wait()
        for j in range(2):
            wide[n, j] = source[j].astype(F32).reshape(tokens * heads, width)
        for h in range(heads):
            rows = stacked(*(head_rows(wide.at[n, j], h, heads) for j in range(2)))
            for i in range(2):
                target[h, i] = rows[i].astype(BF16)


def first_kernel(exchange, order, given_ref, k_heads, v_heads, *refs):
    _, heads, tokens = given_ref.shape
    beta_ref, decay_ref = given_ref.at[:2], given_ref.at[2]
    half = tokens // 2
    out_refs, (sol_ref, row_ref) = refs[: len(order)], refs[len(order) :]
    run = running_rows(decay_ref)
    run_half = doubled(run, half)
    beta_half = stacked_beta(beta_ref, half)
    for i in range(2):
        row_ref[i] = run_half[i]
        row_ref[2 + i] = beta_half[i]
    row_ref[4] = jnp.broadcast_to(run[:, tokens - 1 :], (heads, 2 * half))
    row_ref[5] = run
    solve_heads(exchange, order, k_heads, v_heads, row_ref, out_refs, sol_ref)


def later_kernel(exchange, order, k_heads, v_heads, row_ref, *refs):
    *out_refs, sol_ref = refs[-1 - len(order) :]
    solve_heads(exchange, order, k_heads, v_heads, row_ref, out_refs, sol_ref)


def solve_heads(exchange, order, k_heads, v_heads, row_ref, out_refs, sol_ref):
    span, width = k_heads.shape[2:]
    half = span // 2
    row_at = lax.broadcasted_iota(jnp.int32, (span, span), 0)
    col_at = lax.broadcasted_iota(jnp.int32, (span, span), 1)
    row_time = 2 * lax.rem(row_at, half) + row_at // half
    col_time = 2 * lax.rem(col_at, half) + col_at // half
    below = col_time < row_time
    apart = jnp.where(below, row_time ^ col_time, 0)
    eye = (row_at == col_at).astype(F32)
    eye_wide = eye[:width, :width]
    left = col_at < half

    places = [(n, u) for n in range(len(order)) for u in range(PER_SLOT)]
    for start in range(0, len(places), HEAD_GROUP):
        chains = []
        for s in places[start : start + HEAD_GROUP]:
            h = head_of(exchange, order[s[0]], s[1])
            keys = [k_heads[h, i] for i in range(2)]
            run_row = [row_ref[i, pl.ds(h, 1), :] for i in range(2)]
            beta_row = [row_ref[2 + i, pl.ds(h, 1), :] for i in range(2)]
            run_col = [column(x) for x in run_row]
            beta_col = [column(x) for x in beta_row]
            last_row = row_ref[4, pl.ds(h, 1), :]
            grams = [dot_nt(x, x) for x in keys]
            inv_row = [lax.rsqrt(jnp.sum(g * eye, 0, keepdims=True) + 1e-06) for g in grams]
            inv_col = [lax.rsqrt(jnp.sum(g * eye, 1, keepdims=True) + 1e-06) for g in grams]
            lowers, inverses = [], []
            for i in range(2):
                spread = jnp.exp(jnp.where(below, run_col[i] - run_row[i], 0.0))
                scaled = grams[i] * inv_row[i] * inv_col[i]
                lower = jnp.where(below, beta_col[i] * spread * scaled, 0.0)
                pair = jnp.where(apart == 1, lower, 0.0)
                step = jnp.where((apart >= 2) & (apart < 4), lower, 0.0)
                by_row = jnp.sum(pair, 1, keepdims=True)
                by_col = jnp.sum(pair, 0, keepdims=True)
                step = jnp.concatenate(
                    [step[:half], step[half:] - by_row[half:] * step[:half]], 0
                )
                swapped = jnp.concatenate([step[:, half:], step[:, :half]], 1)
                step = step - jnp.where(left, swapped * by_col, 0.0)
                lowers.append(lower)
                inverses.append(eye - pair - step)
            cross = dot_nt(keys[1], keys[0]) * inv_row[0] * inv_col[1]
            cross = cross * beta_col[1] * jnp.exp(run_col[1] - run_row[0])
            chains.append(
                dict(
                    s=s, h=h, keys=keys, run_row=run_row, beta_row=beta_row,
                    run_col=run_col, last_row=last_row, inv_row=inv_row, inv_col=inv_col,
                    lowers=lowers, inverses=inverses, cross=cross,
                )
            )
        size = 4
        while size < span:
            top = min(4 * size, span)
            for c in chains:
                c["parts"] = [split(x) for x in c["inverses"]]
                c["steps"] = [
                    split(
                        dot_wide(
                            part, split(jnp.where((apart >= size) & (apart < top), low, 0.0))
                        )
                    )
                    for low, part in zip(c["lowers"], c["parts"])
                ]
            for c in chains:
                c["inverses"] = [
                    x - dot_wide(step, part)
                    for x, step, part in zip(c["inverses"], c["steps"], c["parts"])
                ]
            if top == 4 * size:
                for c in chains:
                    c["steps"] = [split(dot_wide(step, step)) for step in c["steps"]]
                for c in chains:
                    c["inverses"] = [
                        x + dot_wide(step, split(x)) for x, step in zip(c["inverses"], c["steps"])
                    ]
            size = top
        for c in chains:
            c["parts"] = [split(x) for x in c["inverses"]]
            c["middle"] = dot_wide(split(c["cross"]), c["parts"][0])
        for c in chains:
            c["corner"] = -dot_wide(c["parts"][1], split(c["middle"]))
        for c in chains:
            values = [v_heads[c["h"], i] for i in range(2)]
            scale_v = c["beta_row"]
            scale_k = [
                b * jnp.exp(r) * n for b, r, n in zip(c["beta_row"], c["run_row"], c["inv_row"])
            ]
            solved = []
            for scale, source in ((scale_k, c["keys"]), (scale_v, values)):
                first = split(c["inverses"][0] * scale[0])
                upper = dot(jnp.concatenate(first, 1), jnp.concatenate([source[0]] * 2, 0))
                corner = split(c["corner"] * scale[0])
                second = split(c["inverses"][1] * scale[1])
                both = jnp.concatenate(source, 0)
                lower = dot(jnp.concatenate([corner[0], second[0]], 1), both) + dot(
                    jnp.concatenate([corner[1], second[1]], 1), both
                )
                solved.append((upper, lower))
            rows = [jnp.concatenate([solved[0][i], solved[1][i]], 1) for i in range(2)]
            c["rows"] = rows
            for i in range(2):
                at = PER_SLOT * c["s"][0] + c["s"][1]
                sol_ref[at, i * span : (i + 1) * span, :] = rows[i]
        for c in chains:
            last_col = column(c["last_row"])
            weighted = []
            for i in range(2):
                remain = jnp.exp(last_col - c["run_col"][i]) * c["inv_col"][i]
                weighted.append(c["rows"][i] * jnp.concatenate([remain, remain], 1))
            high, low = split(jnp.concatenate(weighted, 0))
            keys = jnp.concatenate(c["keys"], 0)
            ends = dot_tn(keys, high) + dot_tn(keys, low)
            gate = jnp.exp(c["last_row"])
            trans = eye_wide * gate - ends[:, :width]
            slot, u = c["s"]
            out_refs[slot][u] = jnp.concatenate([trans, ends[:, width:]], 1).astype(BF16)


def stacked_beta(beta_ref, half):
    first, second = beta_ref[0], beta_ref[1]
    return [
        jnp.concatenate(
            [first[:, i * half : (i + 1) * half], second[:, i * half : (i + 1) * half]], 1
        )
        for i in range(2)
    ]


def queries_kernel(q_ref, *refs):
    out_ref, q_all = refs[-2:]
    tokens, heads, width = q_ref.shape
    q_all[...] = q_ref[...].astype(F32).reshape(tokens * heads, width)
    for h in range(heads):
        out_ref[h] = head_rows(q_all, h, heads).astype(BF16)


def mixing_kernel(exchange, orders, q_heads, k_heads, row_ref, *refs):
    sol_refs, out_ref = refs[: len(orders)], refs[-1]
    heads, tokens, width = q_heads.shape
    half = tokens // 2
    span = 2 * half
    token_at = lax.broadcasted_iota(jnp.int32, (tokens, 2 * span), 0)
    row_at = lax.broadcasted_iota(jnp.int32, (tokens, 2 * span), 1)
    seen = (row_at // span) * half + lax.rem(row_at, half) <= token_at
    row_at = lax.broadcasted_iota(jnp.int32, (span, span), 0)
    col_at = lax.broadcasted_iota(jnp.int32, (span, span), 1)
    eye = (row_at == col_at).astype(F32)

    def one_head(sol_ref, s, at, h):
        queries = q_heads[h].astype(F32)
        keys = [k_heads[h, i] for i in range(2)]
        run_col = column(row_ref[5, pl.ds(h, 1), :])
        run_row = jnp.concatenate([row_ref[i, pl.ds(h, 1), :] for i in range(2)], 1)
        inv_row = [
            lax.rsqrt(jnp.sum(dot_nt(x, x) * eye, 0, keepdims=True) + 1e-06) for x in keys
        ]
        inv_q = lax.rsqrt(jnp.sum(queries * queries, 1, keepdims=True) + 1e-06)
        inner = dot_nt(queries.astype(BF16), jnp.concatenate(keys, 0))
        spread = jnp.concatenate([run_col, run_col], 1) - run_row
        mixing = inner * inv_q * jnp.concatenate(inv_row, 1)
        mixing = jnp.where(seen, jnp.exp(jnp.where(seen, spread, 0.0)) * mixing, 0.0)
        mix_high, mix_low = split(mixing)
        sol_high, sol_low = split(sol_ref[s])
        mixed = dot(mix_high, sol_high) + dot(mix_low, sol_high) + dot(mix_high, sol_low)
        tilde = jnp.exp(run_col) * (queries * inv_q) - mixed[:, :width]
        out_ref[at] = jnp.concatenate([tilde, mixed[:, width:]], 1)

    at = 0
    for order, sol_ref in zip(orders, sol_refs):
        for n, slot in enumerate(order):
            for u in range(PER_SLOT):
                one_head(sol_ref, PER_SLOT * n + u, at, head_of(exchange, slot, u))
                at += 1


def chain_kernel(order, *refs):
    group = len(order)
    term_refs, (local_ref, prefix_ref, end_ref) = refs[:group], refs[group : group + 3]
    held = refs[group + 3]
    width = term_refs[0].shape[1]
    me = lax.rem(lax.axis_index("seq"), group)
    for n, s in enumerate(order):
        held[s] = term_refs[n][...]
    states, prefixes = [], []
    for u in range(PER_SLOT):
        first = held[me, u]
        states.append(first[:, width:].astype(F32))
        prefixes.append(first[:, :width].astype(F32))
    for k in range(1, group):
        for u in range(PER_SLOT):
            local_ref[k - 1, u] = states[u]
            prefix_ref[k - 1, u] = prefixes[u]
        blocks = [held[me ^ k, u] for u in range(PER_SLOT)]
        both = [
            dot(block[:, :width], jnp.concatenate([*split(state), *split(prefix)], 1))
            for block, state, prefix in zip(blocks, states, prefixes)
        ]
        states = [
            x[:, :width] + x[:, width : 2 * width] + block[:, width:].astype(F32)
            for x, block in zip(both, blocks)
        ]
        prefixes = [x[:, 2 * width : 3 * width] + x[:, 3 * width :] for x in both]
    for u in range(PER_SLOT):
        end_ref[u] = states[u].astype(BF16)


def entry_kernel(group, local_ref, prefix_ref, before_ref, *refs):
    out_refs, held = refs[:group], refs[group]
    me = lax.rem(lax.axis_index("seq"), group)
    for u in range(PER_SLOT):
        before = before_ref[u]
        held[0, u] = before
        for k in range(1, group):
            high, low = split(prefix_ref[k - 1, u])
            state = dot(
                jnp.concatenate([high, low], 1), jnp.concatenate([before, before], 0)
            ) + local_ref[k - 1, u]
            held[k, u] = state.astype(BF16)
    for s in range(group):
        out_refs[s][...] = held[me ^ s]


def emit_kernel(exchange, order, slots, mixed_ref, gain_ref, residual_ref, *refs):
    width = mixed_ref.shape[2] // 2
    state_refs, out_ref = refs[: len(slots)], refs[len(slots)]
    for n, slot in enumerate(slots):
        for u in range(PER_SLOT):
            h = head_of(exchange, slot, u)
            mixed = mixed_ref[PER_SLOT * order.index(slot) + u]
            state = state_refs[n][u]
            out = dot(
                jnp.concatenate(split(mixed[:, :width]), 1), jnp.concatenate([state, state], 0)
            ) + mixed[:, width:]
            scale = lax.rsqrt(jnp.mean(out * out, 1, keepdims=True) + 1e-05)
            out = out * scale * gain_ref[...]
            columns = pl.ds(pl.multiple_of(h * width, width), width)
            out_ref[PER_SLOT * n + u] = (
                residual_ref[:, columns].astype(F32) + out
            ).astype(BF16)


def ffn_kernel(count, exchange, pieces, gain_ref, up_at, up_ref, down_ref, *refs):
    given, (act, *outs, tiles_in) = refs[: count * len(pieces)], refs[count * len(pieces) :]
    groups, kept, side, _ = up_ref.shape
    tiles, tokens, _ = tiles_in.shape
    each = tiles // count
    me = lax.axis_index("tensor")
    squares = jnp.zeros((tokens, side), F32)
    for n, part in enumerate(given):
        base = (me ^ (n // len(pieces))) * each
        for i, slot in enumerate(pieces[n % len(pieces)]):
            for u in range(PER_SLOT):
                tile = base + head_of(exchange, slot, u)
                wide = part[PER_SLOT * i + u].astype(F32)
                squares += wide * wide
                tiles_in[tile] = (wide * gain_ref[pl.ds(tile, 1), :]).astype(BF16)
    scale = lax.rsqrt(jnp.sum(squares, 1, keepdims=True) / (tiles * side) + 1e-05)
    scale = jnp.broadcast_to(scale, (tokens, side))
    for c in range(groups):
        picked = jnp.concatenate([tiles_in[up_at[c, j]] for j in range(kept)], 1)
        pre = dot(picked, up_ref[c].reshape(kept * side, side))
        act[:, c * side : (c + 1) * side] = jax.nn.gelu(pre * scale).astype(BF16)
    down_sums(range(count - 1, 0, -1), down_ref, act, outs)


def down_sums(ms, down_ref, act_ref, outs):
    given = act_ref[...]
    for m, out in zip(ms, outs):
        each, _, side = out.shape
        for b in range(0, each, 2):
            pair = jnp.concatenate([down_ref[m * each + b], down_ref[m * each + b + 1]], 1)
            both = dot(given, pair).astype(BF16)
            out[b] = both[:, :side]
            out[b + 1] = both[:, side:]


def own_down_kernel(down_ref, act_ref, after_ref, out_ref):
    down_sums([0], down_ref, act_ref, [out_ref])


def relay_kernel(given_ref, after_ref, out_ref):
    out_ref[...] = given_ref[...]


def dense_kernel(count, at_ref, tiles_ref, after_ref, out_ref):
    groups, kept, side, _ = tiles_ref.shape
    tiles, rows, _ = out_ref.shape
    each = tiles // count
    me = lax.axis_index("tensor")

    def clear(n, carry):
        out_ref[n] = jnp.zeros((rows, side), BF16)
        return carry

    def place(c, carry):
        hidden = pl.ds(pl.multiple_of(c * side, side), side)
        for j in range(kept):
            at = at_ref[c, j]
            out_ref[((at // each) ^ me) * each + lax.rem(at, each), hidden] = tiles_ref[c, j]
        return carry

    lax.fori_loop(0, tiles, clear, 0, unroll=4)
    lax.fori_loop(0, groups, place, 0, unroll=2)


def final_kernel(exchange, pieces, *refs):
    given, sums, out_ref = refs[: len(pieces)], refs[len(pieces) : -1], refs[-1]
    side = given[0].shape[2]
    for part, slots in zip(given, pieces):
        for i, slot in enumerate(slots):
            for u in range(PER_SLOT):
                tile = head_of(exchange, slot, u)
                total = sums[0][tile].astype(F32)
                for ref in sums[1:]:
                    total += ref[tile].astype(F32)
                columns = pl.ds(pl.multiple_of(tile * side, side), side)
                out_ref[:, columns] = (
                    part[PER_SLOT * i + u].astype(F32) + total
                ).astype(BF16)


def local_call(kernel, out_shape, ins, args, scratch=(), flops=0, moved=0, limit=8 * MIB):
    return pl.pallas_call(
        kernel,
        out_shape=out_shape,
        in_specs=ins,
        out_specs=jax.tree.map(lambda _: VMEM, out_shape),
        scratch_shapes=scratch,
        compiler_params=pltpu.CompilerParams(vmem_limit_bytes=limit),
        cost_estimate=pl.CostEstimate(flops=flops, bytes_accessed=moved, transcendentals=0),
    )(*args)


def prefix_states(terms):
    count, index = lax.axis_size("seq"), lax.axis_index("seq")
    own = jnp.stack([terms[s] for s in sorted(terms)])
    everything = lax.all_gather(own, "seq")
    width = own.shape[2]

    def step(k, state):
        block = everything[k]
        new = jnp.einsum(
            "sude,suef->sudf",
            block[..., :width].astype(F32),
            state,
            precision=lax.Precision.HIGHEST,
        ) + block[..., width:].astype(F32)
        return jnp.where(k < index, new, state)

    start = jnp.zeros((*own.shape[:3], width), F32)
    states = lax.fori_loop(0, count, step, start).astype(BF16)
    return {s: states[s] for s in range(len(terms))}


def per_device(
    queries, keys, values, beta, decay, out_gain, residual, ffn_gain,
    up_blocks, up_index, down_kept_tiles, down_index,
):
    tokens, heads, width = queries.shape
    seq_count, tensor_count = lax.axis_size("seq"), lax.axis_size("tensor")
    slots = heads // PER_SLOT
    exchange = slots if seq_count == 2 * slots and slots & (slots - 1) == 0 else 0
    order = sorted(range(slots), key=lambda s: -(s & 1) * slots - s)
    cuts = [0, *(n for n in CUTS if n < slots), slots]
    orders = [order[n:m] for n, m in zip(cuts, cuts[1:])]
    swaps = [[(k, k ^ s) for k in range(seq_count)] for s in range(slots)]
    term = jax.ShapeDtypeStruct((PER_SLOT, width, 2 * width), BF16)
    by_head = jax.ShapeDtypeStruct((heads, 2, tokens, width), BF16)
    rows = jax.ShapeDtypeStruct((6, heads, tokens), F32)
    terms, solved, arrived = {}, [], {}
    for part in orders:
        solution_rows = jax.ShapeDtypeStruct(
            (PER_SLOT * len(part), 2 * tokens, 2 * width), F32
        )
        outs = [term] * len(part) + [solution_rows]
        if not terms:
            k_heads, v_heads = local_call(
                sort_kernel,
                [by_head, by_head],
                [ANY] * 2,
                (keys, values),
                [
                    pltpu.VMEM(keys.shape, BF16),
                    pltpu.VMEM(values.shape, BF16),
                    pltpu.VMEM((2, 2, tokens * heads, width), F32),
                    pltpu.SemaphoreType.DMA((2,)),
                ],
                limit=FIRST_LIMIT,
            )
            *given, sol, row_terms = local_call(
                functools.partial(first_kernel, exchange, part),
                outs + [rows],
                [VMEM] * 3,
                (jnp.concatenate([beta, decay[None]]), k_heads, v_heads),
                flops=3_000_000_000,
                limit=16 * MIB,
            )
        else:
            first = [arrived[order[0]]] if part == order[-1:] and arrived else []
            *given, sol = local_call(
                functools.partial(later_kernel, exchange, part),
                outs,
                [VMEM] * 3 + [ANY] * len(first),
                (k_heads, v_heads, row_terms, *first),
                flops=4_000_000_000,
            )
        terms.update(zip(part, given))
        solved.append(sol)
        if exchange:
            for s in part:
                arrived[s] = lax.ppermute(terms[s], "seq", swaps[s]) if s else terms[s]
    groups, _, side, _ = up_blocks.shape
    tiles = heads * tensor_count
    state = jax.ShapeDtypeStruct((PER_SLOT, width, width), BF16)
    q_heads = local_call(
        queries_kernel,
        jax.ShapeDtypeStruct((heads, tokens, width), BF16),
        [VMEM] + [ANY] * len(orders),
        (queries, *solved),
        [pltpu.VMEM((tokens * heads, width), F32)],
        flops=3_000_000_000,
    )

    def densely(after):
        return local_call(
            functools.partial(dense_kernel, tensor_count),
            jax.ShapeDtypeStruct((tiles, groups * side, side), BF16),
            [SMEM, VMEM, ANY],
            (down_index, down_kept_tiles, after),
            flops=3_000_000_000,
        )

    def mix(after):
        return local_call(
            functools.partial(mixing_kernel, exchange, orders),
            jax.ShapeDtypeStruct((heads, tokens, 2 * width), F32),
            [VMEM] * (3 + len(orders)) + [ANY],
            (q_heads, k_heads, row_terms, *solved, after),
            flops=3_000_000_000,
        )

    if exchange:
        late = order[-1:] + order[:-1]
        inner = jax.ShapeDtypeStruct((slots - 1, PER_SLOT, width, width), F32)
        local, prefix, end = local_call(
            functools.partial(chain_kernel, late),
            [inner, inner, state],
            [VMEM] * slots,
            [arrived[s] for s in late],
            [pltpu.VMEM((slots, PER_SLOT, width, 2 * width), BF16)],
        )
        mixed = mix(end)
        before = lax.ppermute(end, "seq", [(k, k + slots) for k in range(slots)])
        outgoing = local_call(
            functools.partial(entry_kernel, slots),
            [state] * slots,
            [VMEM] * 3,
            (local, prefix, before),
            [pltpu.VMEM((slots, PER_SLOT, width, width), BF16)],
        )
        states = {0: outgoing[0]}
        for s in order[:-1]:
            states[s] = lax.ppermute(outgoing[s], "seq", swaps[s])
    else:
        states = prefix_states(terms)
        mixed = mix(terms[0])
    pieces = PIECES if exchange and slots == 4 else [list(range(slots))]
    hidden = [
        local_call(
            functools.partial(emit_kernel, exchange, order, piece),
            jax.ShapeDtypeStruct((PER_SLOT * len(piece), tokens, width), BF16),
            [VMEM] * (3 + len(piece)),
            (mixed, out_gain.reshape(1, width), residual, *(states[s] for s in piece)),
        )
        for piece in pieces
    ]

    flips = {
        d: [(k, k ^ d) for k in range(tensor_count)]
        for d in (1 << b for b in range(tensor_count.bit_length() - 1))
    }
    down_dense = densely(hidden[0])
    parts = [{0: given} for given in hidden]
    for held in parts:
        for d in sorted(flips, reverse=True):
            for m in list(held):
                sent = held[m]
                if m and d == 1:
                    sent = local_call(
                        relay_kernel,
                        jax.ShapeDtypeStruct(sent.shape, sent.dtype),
                        [VMEM, ANY],
                        (sent, down_dense),
                    )
                held[m | d] = lax.ppermute(sent, "tensor", flips[d])
    part = jax.ShapeDtypeStruct((heads, tokens, side), BF16)
    others = list(range(tensor_count - 1, 0, -1))
    act, *sums = local_call(
        functools.partial(ffn_kernel, tensor_count, exchange, pieces),
        [jax.ShapeDtypeStruct((tokens, groups * side), BF16)] + [part] * len(others),
        [VMEM, SMEM, VMEM, VMEM] + [VMEM] * (tensor_count * len(pieces)),
        (
            ffn_gain.reshape(tiles, side), up_index, up_blocks, down_dense,
            *(held[m] for m in range(tensor_count) for held in parts),
        ),
        [pltpu.VMEM((tiles, tokens, side), BF16)],
        limit=12 * MIB,
    )
    held = {m: [given] for m, given in zip(others, sums)}
    for d in sorted(flips):
        for m in sorted(m for m in held if not m & d and m | d in held):
            held[m].append(lax.ppermute(added(held.pop(m | d)), "tensor", flips[d]))
    crossing = {m: added(held[m]) for m in held}
    own = local_call(
        own_down_kernel, part, [VMEM, VMEM, ANY], (down_dense, act, crossing[max(crossing)]),
        flops=1_000_000_000,
    )
    moved = [own] + [
        lax.ppermute(crossing[m], "tensor", flips[m]) for m in sorted(crossing)
    ]
    return local_call(
        functools.partial(final_kernel, exchange, pieces),
        jax.ShapeDtypeStruct((tokens, heads * side), BF16),
        [VMEM] * (len(pieces) + len(moved)),
        (*hidden, *moved),
    )


def added(terms):
    if len(terms) == 1:
        return terms[0]
    return sum(term.astype(F32) for term in terms).astype(BF16)


def solution(mesh):
    placed = (
        P("seq", "tensor", None),
        P(None, "seq", "tensor", None),
        P(None, "seq", "tensor", None),
        P(None, "tensor", "seq"),
        P("tensor", "seq"),
        P(),
        P("seq", "tensor"),
        P(),
        P("tensor", None, None, None),
        P("tensor", None),
        P("tensor", None, None, None),
        P("tensor", None),
    )
    return jax.shard_map(
        per_device, mesh=mesh, in_specs=placed, out_specs=P("seq", "tensor"), check_vma=False
    )
```

```python
import functools

import jax
import jax.numpy as jnp
from jax import lax
from jax.experimental import pallas as pl
from jax.experimental.pallas import tpu as pltpu
from jax.sharding import PartitionSpec as P

F32 = jnp.float32
BF16 = jnp.bfloat16
HEAD_GROUP = 6
PER_SLOT = 2
CUTS = (1, 3)
PIECES = [[0, 1, 2, 3]]
FIRST_LIMIT = 52 * (1 << 20) + (1 << 19)
MIB = 1 << 20
VMEM = pl.BlockSpec(memory_space=pltpu.VMEM)
SMEM = pl.BlockSpec(memory_space=pltpu.SMEM)
ANY = pl.BlockSpec(memory_space=pl.ANY)


def dot(a, b):
    return jnp.dot(a, b, preferred_element_type=F32)


def dot_nt(a, b):
    return lax.dot_general(a, b, (((1,), (1,)), ((), ())), preferred_element_type=F32)


def dot_tn(a, b):
    return lax.dot_general(a, b, (((0,), (0,)), ((), ())), preferred_element_type=F32)


def split(x):
    high = x.astype(BF16)
    return high, (x - high.astype(F32)).astype(BF16)


def dot_wide(a, b):
    width = a[0].shape[1]
    row = jnp.concatenate([b[0], b[1]], 1)
    out = dot(jnp.concatenate([a[0], a[1]], 1), jnp.concatenate([row, row], 0))
    return out[:, :width] + out[:, width:]


def column(row):
    n = row.shape[1]
    return jnp.broadcast_to(row, (n, n)).T


def head_rows(ref, h, heads):
    return ref[pl.ds(h, ref.shape[0] // heads - 1, stride=heads), :]


def stacked(first, second):
    half = first.shape[0] // 2
    return [
        jnp.concatenate([first[i * half : (i + 1) * half], second[i * half : (i + 1) * half]], 0)
        for i in range(2)
    ]


def running_rows(decay_ref):
    tokens = decay_ref.shape[1]
    earlier = lax.broadcasted_iota(jnp.int32, (tokens, tokens), 0)
    later = lax.broadcasted_iota(jnp.int32, (tokens, tokens), 1)
    return jnp.dot(
        decay_ref[...],
        (earlier <= later).astype(F32),
        preferred_element_type=F32,
        precision=lax.Precision.HIGHEST,
    )


def doubled(rows, half):
    return [
        jnp.concatenate([rows[:, i * half : (i + 1) * half]] * 2, 1) for i in range(2)
    ]


def head_of(exchange, slot, u):
    if exchange:
        return PER_SLOT * (lax.rem(lax.axis_index("seq"), exchange) ^ slot) + u
    return PER_SLOT * slot + u


def sort_kernel(k_hbm, v_hbm, k_heads, v_heads, k_ref, v_ref, wide, sems):
    _, tokens, heads, width = k_hbm.shape
    copies = [
        pltpu.make_async_copy(source, target, sems.at[n])
        for n, (source, target) in enumerate(((k_hbm, k_ref), (v_hbm, v_ref)))
    ]
    for copy in copies:
        copy.start()
    for n, (source, target) in enumerate(((k_ref, k_heads), (v_ref, v_heads))):
        copies[n].wait()
        for j in range(2):
            wide[n, j, : tokens * heads] = source[j].astype(F32).reshape(tokens * heads, width)
        for h in range(heads):
            rows = stacked(*(head_rows(wide.at[n, j], h, heads) for j in range(2)))
            for i in range(2):
                target[h, i] = rows[i].astype(BF16)


def first_kernel(exchange, order, given_ref, k_heads, v_heads, *refs):
    _, heads, tokens = given_ref.shape
    beta_ref, decay_ref = given_ref.at[:2], given_ref.at[2]
    half = tokens // 2
    out_refs, (sol_ref, row_ref) = refs[: len(order)], refs[len(order) :]
    run = running_rows(decay_ref)
    run_half = doubled(run, half)
    beta_half = stacked_beta(beta_ref, half)
    for i in range(2):
        row_ref[i] = run_half[i]
        row_ref[2 + i] = beta_half[i]
    row_ref[4] = jnp.broadcast_to(run[:, tokens - 1 :], (heads, 2 * half))
    row_ref[5] = run
    solve_heads(exchange, order, k_heads, v_heads, row_ref, out_refs, sol_ref)


def later_kernel(exchange, order, k_heads, v_heads, row_ref, *refs):
    *out_refs, sol_ref = refs[-1 - len(order) :]
    solve_heads(exchange, order, k_heads, v_heads, row_ref, out_refs, sol_ref)


def solve_heads(exchange, order, k_heads, v_heads, row_ref, out_refs, sol_ref):
    span, width = k_heads.shape[2:]
    half = span // 2
    row_at = lax.broadcasted_iota(jnp.int32, (span, span), 0)
    col_at = lax.broadcasted_iota(jnp.int32, (span, span), 1)
    row_time = 2 * lax.rem(row_at, half) + row_at // half
    col_time = 2 * lax.rem(col_at, half) + col_at // half
    below = col_time < row_time
    apart = jnp.where(below, row_time ^ col_time, 0)
    eye = (row_at == col_at).astype(F32)
    eye_wide = eye[:width, :width]
    left = col_at < half

    places = [(n, u) for n in range(len(order)) for u in range(PER_SLOT)]
    for start in range(0, len(places), HEAD_GROUP):
        chains = []
        for s in places[start : start + HEAD_GROUP]:
            h = head_of(exchange, order[s[0]], s[1])
            keys = [k_heads[h, i] for i in range(2)]
            run_row = [row_ref[i, pl.ds(h, 1), :] for i in range(2)]
            beta_row = [row_ref[2 + i, pl.ds(h, 1), :] for i in range(2)]
            run_col = [column(x) for x in run_row]
            beta_col = [column(x) for x in beta_row]
            last_row = row_ref[4, pl.ds(h, 1), :]
            grams = [dot_nt(x, x) for x in keys]
            inv_row = [lax.rsqrt(jnp.sum(g * eye, 0, keepdims=True) + 1e-06) for g in grams]
            inv_col = [lax.rsqrt(jnp.sum(g * eye, 1, keepdims=True) + 1e-06) for g in grams]
            lowers, inverses = [], []
            for i in range(2):
                spread = jnp.exp(jnp.where(below, run_col[i] - run_row[i], 0.0))
                scaled = grams[i] * inv_row[i] * inv_col[i]
                lower = jnp.where(below, beta_col[i] * spread * scaled, 0.0)
                pair = jnp.where(apart == 1, lower, 0.0)
                step = jnp.where((apart >= 2) & (apart < 4), lower, 0.0)
                by_row = jnp.sum(pair, 1, keepdims=True)
                by_col = jnp.sum(pair, 0, keepdims=True)
                step = jnp.concatenate(
                    [step[:half], step[half:] - by_row[half:] * step[:half]], 0
                )
                swapped = jnp.concatenate([step[:, half:], step[:, :half]], 1)
                step = step - jnp.where(left, swapped * by_col, 0.0)
                lowers.append(lower)
                inverses.append(eye - pair - step)
            cross = dot_nt(keys[1], keys[0]) * inv_row[0] * inv_col[1]
            cross = cross * beta_col[1] * jnp.exp(run_col[1] - run_row[0])
            chains.append(
                dict(
                    s=s, h=h, keys=keys, run_row=run_row, beta_row=beta_row,
                    run_col=run_col, last_row=last_row, inv_row=inv_row, inv_col=inv_col,
                    lowers=lowers, inverses=inverses, cross=cross,
                )
            )
        size = 4
        while size < span:
            top = min(4 * size, span)
            for c in chains:
                c["parts"] = [split(x) for x in c["inverses"]]
                c["steps"] = [
                    split(
                        dot_wide(
                            part, split(jnp.where((apart >= size) & (apart < top), low, 0.0))
                        )
                    )
                    for low, part in zip(c["lowers"], c["parts"])
                ]
            for c in chains:
                c["inverses"] = [
                    x - dot_wide(step, part)
                    for x, step, part in zip(c["inverses"], c["steps"], c["parts"])
                ]
            if top == 4 * size:
                for c in chains:
                    c["steps"] = [split(dot_wide(step, step)) for step in c["steps"]]
                for c in chains:
                    c["inverses"] = [
                        x + dot_wide(step, split(x)) for x, step in zip(c["inverses"], c["steps"])
                    ]
            size = top
        for c in chains:
            c["parts"] = [split(x) for x in c["inverses"]]
            c["middle"] = dot_wide(split(c["cross"]), c["parts"][0])
        for c in chains:
            c["corner"] = -dot_wide(c["parts"][1], split(c["middle"]))
        for c in chains:
            values = [v_heads[c["h"], i] for i in range(2)]
            scale_v = c["beta_row"]
            scale_k = [
                b * jnp.exp(r) * n for b, r, n in zip(c["beta_row"], c["run_row"], c["inv_row"])
            ]
            solved = []
            for scale, source in ((scale_k, c["keys"]), (scale_v, values)):
                first = split(c["inverses"][0] * scale[0])
                upper = dot(jnp.concatenate(first, 1), jnp.concatenate([source[0]] * 2, 0))
                corner = split(c["corner"] * scale[0])
                second = split(c["inverses"][1] * scale[1])
                both = jnp.concatenate(source, 0)
                lower = dot(jnp.concatenate([corner[0], second[0]], 1), both) + dot(
                    jnp.concatenate([corner[1], second[1]], 1), both
                )
                solved.append((upper, lower))
            rows = [jnp.concatenate([solved[0][i], solved[1][i]], 1) for i in range(2)]
            c["rows"] = rows
            for i in range(2):
                at = PER_SLOT * c["s"][0] + c["s"][1]
                sol_ref[at, i * span : (i + 1) * span, :] = rows[i]
        for c in chains:
            last_col = column(c["last_row"])
            weighted = []
            for i in range(2):
                remain = jnp.exp(last_col - c["run_col"][i]) * c["inv_col"][i]
                weighted.append(c["rows"][i] * jnp.concatenate([remain, remain], 1))
            high, low = split(jnp.concatenate(weighted, 0))
            keys = jnp.concatenate(c["keys"], 0)
            ends = dot_tn(keys, high) + dot_tn(keys, low)
            gate = jnp.exp(c["last_row"])
            trans = eye_wide * gate - ends[:, :width]
            slot, u = c["s"]
            out_refs[slot][u] = jnp.concatenate([trans, ends[:, width:]], 1).astype(BF16)


def stacked_beta(beta_ref, half):
    first, second = beta_ref[0], beta_ref[1]
    return [
        jnp.concatenate(
            [first[:, i * half : (i + 1) * half], second[:, i * half : (i + 1) * half]], 1
        )
        for i in range(2)
    ]


def queries_kernel(q_ref, *refs):
    out_ref, q_all = refs[-2:]
    tokens, heads, width = q_ref.shape
    q_all[: tokens * heads] = q_ref[...].astype(F32).reshape(tokens * heads, width)
    for h in range(heads):
        out_ref[h] = head_rows(q_all, h, heads).astype(BF16)


def mixing_kernel(exchange, orders, q_heads, k_heads, row_ref, *refs):
    sol_refs, out_ref = refs[: len(orders)], refs[-1]
    heads, tokens, width = q_heads.shape
    half = tokens // 2
    span = 2 * half
    token_at = lax.broadcasted_iota(jnp.int32, (tokens, 2 * span), 0)
    row_at = lax.broadcasted_iota(jnp.int32, (tokens, 2 * span), 1)
    seen = (row_at // span) * half + lax.rem(row_at, half) <= token_at
    row_at = lax.broadcasted_iota(jnp.int32, (span, span), 0)
    col_at = lax.broadcasted_iota(jnp.int32, (span, span), 1)
    eye = (row_at == col_at).astype(F32)

    def one_head(sol_ref, s, at, h):
        queries = q_heads[h].astype(F32)
        keys = [k_heads[h, i] for i in range(2)]
        run_col = column(row_ref[5, pl.ds(h, 1), :])
        run_row = jnp.concatenate([row_ref[i, pl.ds(h, 1), :] for i in range(2)], 1)
        inv_row = [
            lax.rsqrt(jnp.sum(dot_nt(x, x) * eye, 0, keepdims=True) + 1e-06) for x in keys
        ]
        inv_q = lax.rsqrt(jnp.sum(queries * queries, 1, keepdims=True) + 1e-06)
        inner = dot_nt(queries.astype(BF16), jnp.concatenate(keys, 0))
        spread = jnp.concatenate([run_col, run_col], 1) - run_row
        mixing = inner * inv_q * jnp.concatenate(inv_row, 1)
        mixing = jnp.where(seen, jnp.exp(jnp.where(seen, spread, 0.0)) * mixing, 0.0)
        mix_high, mix_low = split(mixing)
        sol_high, sol_low = split(sol_ref[s])
        mixed = dot(mix_high, sol_high) + dot(mix_low, sol_high) + dot(mix_high, sol_low)
        tilde = jnp.exp(run_col) * (queries * inv_q) - mixed[:, :width]
        out_ref[at] = jnp.concatenate([tilde, mixed[:, width:]], 1)

    at = 0
    for order, sol_ref in zip(orders, sol_refs):
        for n, slot in enumerate(order):
            for u in range(PER_SLOT):
                one_head(sol_ref, PER_SLOT * n + u, at, head_of(exchange, slot, u))
                at += 1


def chain_kernel(order, *refs):
    group = len(order)
    term_refs, (local_ref, prefix_ref, end_ref) = refs[:group], refs[group : group + 3]
    held = refs[group + 3]
    width = term_refs[0].shape[1]
    me = lax.rem(lax.axis_index("seq"), group)
    for n, s in enumerate(order):
        held[s] = term_refs[n][...]
    states, prefixes = [], []
    for u in range(PER_SLOT):
        first = held[me, u]
        states.append(first[:, width:].astype(F32))
        prefixes.append(first[:, :width].astype(F32))
    for k in range(1, group):
        for u in range(PER_SLOT):
            local_ref[k - 1, u] = states[u]
            prefix_ref[k - 1, u] = prefixes[u]
        blocks = [held[me ^ k, u] for u in range(PER_SLOT)]
        both = [
            dot(block[:, :width], jnp.concatenate([*split(state), *split(prefix)], 1))
            for block, state, prefix in zip(blocks, states, prefixes)
        ]
        states = [
            x[:, :width] + x[:, width : 2 * width] + block[:, width:].astype(F32)
            for x, block in zip(both, blocks)
        ]
        prefixes = [x[:, 2 * width : 3 * width] + x[:, 3 * width :] for x in both]
    for u in range(PER_SLOT):
        end_ref[u] = states[u].astype(BF16)


def entry_kernel(group, local_ref, prefix_ref, before_ref, *refs):
    out_refs, held = refs[:group], refs[group]
    me = lax.rem(lax.axis_index("seq"), group)
    for u in range(PER_SLOT):
        before = before_ref[u]
        held[0, u] = before
        for k in range(1, group):
            high, low = split(prefix_ref[k - 1, u])
            state = dot(
                jnp.concatenate([high, low], 1), jnp.concatenate([before, before], 0)
            ) + local_ref[k - 1, u]
            held[k, u] = state.astype(BF16)
    for s in range(group):
        out_refs[s][...] = held[me ^ s]


def emit_kernel(exchange, order, slots, mixed_ref, gain_ref, residual_ref, *refs):
    width = mixed_ref.shape[2] // 2
    state_refs, out_ref = refs[: len(slots)], refs[len(slots)]
    for n, slot in enumerate(slots):
        for u in range(PER_SLOT):
            h = head_of(exchange, slot, u)
            mixed = mixed_ref[PER_SLOT * order.index(slot) + u]
            state = state_refs[n][u]
            out = dot(
                jnp.concatenate(split(mixed[:, :width]), 1), jnp.concatenate([state, state], 0)
            ) + mixed[:, width:]
            scale = lax.rsqrt(jnp.mean(out * out, 1, keepdims=True) + 1e-05)
            out = out * scale * gain_ref[...]
            columns = pl.ds(pl.multiple_of(h * width, width), width)
            out_ref[PER_SLOT * n + u] = (
                residual_ref[:, columns].astype(F32) + out
            ).astype(BF16)


def ffn_kernel(count, exchange, pieces, gain_ref, up_at, up_ref, down_ref, *refs):
    given, (act, *outs, tiles_in) = refs[: count * len(pieces)], refs[count * len(pieces) :]
    groups, kept, side, _ = up_ref.shape
    tiles, tokens, _ = tiles_in.shape
    each = tiles // count
    me = lax.axis_index("tensor")
    squares = jnp.zeros((tokens, side), F32)
    for n, part in enumerate(given):
        base = (me ^ (n // len(pieces))) * each
        for i, slot in enumerate(pieces[n % len(pieces)]):
            for u in range(PER_SLOT):
                tile = base + head_of(exchange, slot, u)
                wide = part[PER_SLOT * i + u].astype(F32)
                squares += wide * wide
                tiles_in[tile] = (wide * gain_ref[pl.ds(tile, 1), :]).astype(BF16)
    scale = lax.rsqrt(jnp.sum(squares, 1, keepdims=True) / (tiles * side) + 1e-05)
    scale = jnp.broadcast_to(scale, (tokens, side))
    for c in range(groups):
        picked = jnp.concatenate([tiles_in[up_at[c, j]] for j in range(kept)], 1)
        pre = dot(picked, up_ref[c].reshape(kept * side, side))
        act[:, c * side : (c + 1) * side] = jax.nn.gelu(pre * scale).astype(BF16)
    down_sums(range(count - 1, 0, -1), down_ref, act, outs)


def down_sums(ms, down_ref, act_ref, outs):
    given = act_ref[...]
    for m, out in zip(ms, outs):
        each, _, side = out.shape
        for b in range(0, each, 2):
            pair = jnp.concatenate([down_ref[m * each + b], down_ref[m * each + b + 1]], 1)
            both = dot(given, pair).astype(BF16)
            out[b] = both[:, :side]
            out[b + 1] = both[:, side:]


def own_down_kernel(down_ref, act_ref, after_ref, out_ref):
    down_sums([0], down_ref, act_ref, [out_ref])


def relay_kernel(given_ref, after_ref, out_ref):
    out_ref[...] = given_ref[...]


def dense_kernel(count, at_ref, tiles_ref, after_ref, out_ref):
    groups, kept, side, _ = tiles_ref.shape
    tiles, rows, _ = out_ref.shape
    each = tiles // count
    me = lax.axis_index("tensor")

    def clear(n, carry):
        out_ref[n] = jnp.zeros((rows, side), BF16)
        return carry

    def place(c, carry):
        hidden = pl.ds(pl.multiple_of(c * side, side), side)
        for j in range(kept):
            at = at_ref[c, j]
            out_ref[((at // each) ^ me) * each + lax.rem(at, each), hidden] = tiles_ref[c, j]
        return carry

    lax.fori_loop(0, tiles, clear, 0, unroll=4)
    lax.fori_loop(0, groups, place, 0, unroll=2)


def final_kernel(exchange, pieces, *refs):
    given, sums, out_ref = refs[: len(pieces)], refs[len(pieces) : -1], refs[-1]
    side = given[0].shape[2]
    for part, slots in zip(given, pieces):
        for i, slot in enumerate(slots):
            for u in range(PER_SLOT):
                tile = head_of(exchange, slot, u)
                total = sums[0][tile].astype(F32)
                for ref in sums[1:]:
                    total += ref[tile].astype(F32)
                columns = pl.ds(pl.multiple_of(tile * side, side), side)
                out_ref[:, columns] = (
                    part[PER_SLOT * i + u].astype(F32) + total
                ).astype(BF16)


def local_call(kernel, out_shape, ins, args, scratch=(), flops=0, moved=0, limit=8 * MIB):
    return pl.pallas_call(
        kernel,
        out_shape=out_shape,
        in_specs=ins,
        out_specs=jax.tree.map(lambda _: VMEM, out_shape),
        scratch_shapes=scratch,
        compiler_params=pltpu.CompilerParams(vmem_limit_bytes=limit),
        cost_estimate=pl.CostEstimate(flops=flops, bytes_accessed=moved, transcendentals=0),
    )(*args)


def prefix_states(terms):
    count, index = lax.axis_size("seq"), lax.axis_index("seq")
    own = jnp.stack([terms[s] for s in sorted(terms)])
    everything = lax.all_gather(own, "seq")
    width = own.shape[2]

    def step(k, state):
        block = everything[k]
        new = jnp.einsum(
            "sude,suef->sudf",
            block[..., :width].astype(F32),
            state,
            precision=lax.Precision.HIGHEST,
        ) + block[..., width:].astype(F32)
        return jnp.where(k < index, new, state)

    start = jnp.zeros((*own.shape[:3], width), F32)
    states = lax.fori_loop(0, count, step, start).astype(BF16)
    return {s: states[s] for s in range(len(terms))}


def per_device(
    queries, keys, values, beta, decay, out_gain, residual, ffn_gain,
    up_blocks, up_index, down_kept_tiles, down_index,
):
    tokens, heads, width = queries.shape
    seq_count, tensor_count = lax.axis_size("seq"), lax.axis_size("tensor")
    slots = heads // PER_SLOT
    exchange = slots if seq_count == 2 * slots and slots & (slots - 1) == 0 else 0
    order = sorted(range(slots), key=lambda s: -(s & 1) * slots - s)
    cuts = [0, *(n for n in CUTS if n < slots), slots]
    orders = [order[n:m] for n, m in zip(cuts, cuts[1:])]
    swaps = [[(k, k ^ s) for k in range(seq_count)] for s in range(slots)]
    term = jax.ShapeDtypeStruct((PER_SLOT, width, 2 * width), BF16)
    by_head = jax.ShapeDtypeStruct((heads, 2, tokens, width), BF16)
    rows = jax.ShapeDtypeStruct((6, heads, tokens), F32)
    terms, solved, arrived = {}, [], {}
    for part in orders:
        solution_rows = jax.ShapeDtypeStruct(
            (PER_SLOT * len(part), 2 * tokens, 2 * width), F32
        )
        outs = [term] * len(part) + [solution_rows]
        if not terms:
            k_heads, v_heads = local_call(
                sort_kernel,
                [by_head, by_head],
                [ANY] * 2,
                (keys, values),
                [
                    pltpu.VMEM(keys.shape, BF16),
                    pltpu.VMEM(values.shape, BF16),
                    pltpu.VMEM((2, 2, (tokens + 1) * heads, width), F32),
                    pltpu.SemaphoreType.DMA((2,)),
                ],
                limit=FIRST_LIMIT,
            )
            *given, sol, row_terms = local_call(
                functools.partial(first_kernel, exchange, part),
                outs + [rows],
                [VMEM] * 3,
                (jnp.concatenate([beta, decay[None]]), k_heads, v_heads),
                flops=3_000_000_000,
                limit=16 * MIB,
            )
        else:
            first = [arrived[order[0]]] if part == order[-1:] and arrived else []
            *given, sol = local_call(
                functools.partial(later_kernel, exchange, part),
                outs,
                [VMEM] * 3 + [ANY] * len(first),
                (k_heads, v_heads, row_terms, *first),
                flops=4_000_000_000,
            )
        terms.update(zip(part, given))
        solved.append(sol)
        if exchange:
            for s in part:
                arrived[s] = lax.ppermute(terms[s], "seq", swaps[s]) if s else terms[s]
    groups, _, side, _ = up_blocks.shape
    tiles = heads * tensor_count
    state = jax.ShapeDtypeStruct((PER_SLOT, width, width), BF16)
    q_heads = local_call(
        queries_kernel,
        jax.ShapeDtypeStruct((heads, tokens, width), BF16),
        [VMEM] + [ANY] * len(orders),
        (queries, *solved),
        [pltpu.VMEM(((tokens + 1) * heads, width), F32)],
        flops=3_000_000_000,
    )

    def densely(after):
        return local_call(
            functools.partial(dense_kernel, tensor_count),
            jax.ShapeDtypeStruct((tiles, groups * side, side), BF16),
            [SMEM, VMEM, ANY],
            (down_index, down_kept_tiles, after),
            flops=3_000_000_000,
        )

    def mix(after):
        return local_call(
            functools.partial(mixing_kernel, exchange, orders),
            jax.ShapeDtypeStruct((heads, tokens, 2 * width), F32),
            [VMEM] * (3 + len(orders)) + [ANY],
            (q_heads, k_heads, row_terms, *solved, after),
            flops=3_000_000_000,
        )

    if exchange:
        late = order[-1:] + order[:-1]
        inner = jax.ShapeDtypeStruct((slots - 1, PER_SLOT, width, width), F32)
        local, prefix, end = local_call(
            functools.partial(chain_kernel, late),
            [inner, inner, state],
            [VMEM] * slots,
            [arrived[s] for s in late],
            [pltpu.VMEM((slots, PER_SLOT, width, 2 * width), BF16)],
        )
        mixed = mix(end)
        before = lax.ppermute(end, "seq", [(k, k + slots) for k in range(slots)])
        outgoing = local_call(
            functools.partial(entry_kernel, slots),
            [state] * slots,
            [VMEM] * 3,
            (local, prefix, before),
            [pltpu.VMEM((slots, PER_SLOT, width, width), BF16)],
        )
        states = {0: outgoing[0]}
        for s in order[:-1]:
            states[s] = lax.ppermute(outgoing[s], "seq", swaps[s])
    else:
        states = prefix_states(terms)
        mixed = mix(terms[0])
    pieces = PIECES if exchange and slots == 4 else [list(range(slots))]
    hidden = [
        local_call(
            functools.partial(emit_kernel, exchange, order, piece),
            jax.ShapeDtypeStruct((PER_SLOT * len(piece), tokens, width), BF16),
            [VMEM] * (3 + len(piece)),
            (mixed, out_gain.reshape(1, width), residual, *(states[s] for s in piece)),
        )
        for piece in pieces
    ]

    flips = {
        d: [(k, k ^ d) for k in range(tensor_count)]
        for d in (1 << b for b in range(tensor_count.bit_length() - 1))
    }
    down_dense = densely(hidden[0])
    parts = [{0: given} for given in hidden]
    for held in parts:
        for d in sorted(flips, reverse=True):
            for m in list(held):
                sent = held[m]
                if m and d == 1:
                    sent = local_call(
                        relay_kernel,
                        jax.ShapeDtypeStruct(sent.shape, sent.dtype),
                        [VMEM, ANY],
                        (sent, down_dense),
                    )
                held[m | d] = lax.ppermute(sent, "tensor", flips[d])
    part = jax.ShapeDtypeStruct((heads, tokens, side), BF16)
    others = list(range(tensor_count - 1, 0, -1))
    act, *sums = local_call(
        functools.partial(ffn_kernel, tensor_count, exchange, pieces),
        [jax.ShapeDtypeStruct((tokens, groups * side), BF16)] + [part] * len(others),
        [VMEM, SMEM, VMEM, VMEM] + [VMEM] * (tensor_count * len(pieces)),
        (
            ffn_gain.reshape(tiles, side), up_index, up_blocks, down_dense,
            *(held[m] for m in range(tensor_count) for held in parts),
        ),
        [pltpu.VMEM((tiles, tokens, side), BF16)],
        limit=12 * MIB,
    )
    held = {m: [given] for m, given in zip(others, sums)}
    for d in sorted(flips):
        for m in sorted(m for m in held if not m & d and m | d in held):
            held[m].append(lax.ppermute(added(held.pop(m | d)), "tensor", flips[d]))
    crossing = {m: added(held[m]) for m in held}
    own = local_call(
        own_down_kernel, part, [VMEM, VMEM, ANY], (down_dense, act, crossing[max(crossing)]),
        flops=1_000_000_000,
    )
    moved = [own] + [
        lax.ppermute(crossing[m], "tensor", flips[m]) for m in sorted(crossing)
    ]
    return local_call(
        functools.partial(final_kernel, exchange, pieces),
        jax.ShapeDtypeStruct((tokens, heads * side), BF16),
        [VMEM] * (len(pieces) + len(moved)),
        (*hidden, *moved),
    )


def added(terms):
    if len(terms) == 1:
        return terms[0]
    return sum(term.astype(F32) for term in terms).astype(BF16)


def solution(mesh):
    placed = (
        P("seq", "tensor", None),
        P(None, "seq", "tensor", None),
        P(None, "seq", "tensor", None),
        P(None, "tensor", "seq"),
        P("tensor", "seq"),
        P(),
        P("seq", "tensor"),
        P(),
        P("tensor", None, None, None),
        P("tensor", None),
        P("tensor", None, None, None),
        P("tensor", None),
    )
    return jax.shard_map(
        per_device, mesh=mesh, in_specs=placed, out_specs=P("seq", "tensor"), check_vma=False
    )
```
